256 devices in a mesh: dp: 8 (over x, core), seq: 32 (over z, y).
Axes of the slice: x: 4, y: 4, z: 8, core: 2. Of those that a mesh axis runs over, the one named last changes fastest.
Arguments:
- query_blocks: bfloat16 [16, 2048, 4096], P('dp', 'seq'), may hold values from -64 to 64
- key_blocks: bfloat16 [16, 2048, 4096], P('dp', 'seq'), may hold values from -6 to 6
- value_blocks: bfloat16 [16, 2048, 4096], P('dp', 'seq'), may hold values from -6 to 6
- value_scales: float32 [16, 2048, 32], P('dp', 'seq'), may hold values from 0.25 to 4
- targets: bfloat16 [16, 2048, 4096], P('dp', 'seq'), may hold values from -41 to 41
- frame_ids: int32 [16, 2048], P('dp', 'seq'), may hold values from 0 to 15, never falling along the last dimension, each value on 1 to 256 neighbouring positions
- bucket_ids: int32 [16], P('dp'), may hold values from 0 to 7
Outputs:
- query_grad: bfloat16 [16, 2048, 4096], P('dp', 'seq')
- key_grad: bfloat16 [16, 2048, 4096], P('dp', 'seq')
- value_grad: bfloat16 [16, 2048, 4096], P('dp', 'seq')
The draws below stay inside these ranges and needn't reach their ends.
Inputs may be any that keep to these rules, and one draw needn't show every extreme that they name: `frame_ids`: frame ids never fall along a sample; each frame holds 1 to 256 tokens.
All inputs are finite; a program needn't handle non-finite values.
Results may differ from the reference program's by a relative error of at most 0.009.
The reference program's roundings to bfloat16 on the way (of `query_rot`, `value_deq`, `probs_low`, `attended`, `cotangent`, `grad_scores` and `grad_query`) count: a program that leaves them out, or rounds other values in their place, can miss the bound.
Values may be sent and summed in bfloat16 or wider, within the bound.
A program may use at most 128 MiB of HBM per device.

```python
import math
import jax
import jax.numpy as jnp
import numpy as np
from jax import lax

HEADS = 32
HD = 128
LEN = 2048
FRAMES = 16
NB = 8
FRAME_MOST = 256
HF = 4096
SAMPLES = 16


def shared_normals(key):
    key_part, query_part, row_part = jax.random.split(key, 3)
    shape = (SAMPLES, LEN, HEADS, HD)
    key_base = jnp.clip(jax.random.normal(key_part, shape, jnp.float32), -6.0, 6.0)
    query_base = jnp.clip(jax.random.normal(query_part, shape, jnp.float32), -6.0, 6.0)
    row_scale = jnp.exp(jax.random.uniform(row_part, (SAMPLES, LEN, 1, 1), jnp.float32, math.log(0.6), math.log(6.0)))
    return (key_base, query_base, row_scale)


def draw_key_blocks(key, part):
    key_base, query_base, row_scale = shared_normals(key)
    result = key_base
    return result.reshape(SAMPLES, LEN, HEADS * HD).astype(jnp.bfloat16)


def draw_query_blocks(key, part):
    key_base, query_base, row_scale = shared_normals(key)
    result = query_base * row_scale
    return result.reshape(SAMPLES, LEN, HEADS * HD).astype(jnp.bfloat16)


def draw_targets(key, part):
    key = jax.random.fold_in(key, 3)
    noise = jnp.clip(jax.random.normal(key, (SAMPLES, LEN, HEADS * HD), jnp.float32), -4.0, 4.0)
    token_scale = 1.0 + 2.0 * jnp.arange(LEN, dtype=jnp.float32) / LEN
    sample_scale = 1.0 + 2.0 * jnp.arange(SAMPLES, dtype=jnp.float32) / SAMPLES
    scale_grid = sample_scale[:, None, None] * token_scale[None, :, None]
    result = noise * scale_grid
    return result.astype(jnp.bfloat16)


def touch_ends(array, own_key, least, largest):
    longest = array.shape.index(max(array.shape))
    spots = []
    for shift in (0, 1):
        where = [jax.random.randint(jax.random.fold_in(own_key, axis), (), 0, length) for axis, length in enumerate(array.shape)]
        where[longest] = (where[longest] + shift) % array.shape[longest]
        spots.append(tuple(where))
    return array.at[spots[0]].set(least).at[spots[1]].set(largest)


def steps_of(key, shape, shards, least, high):
    gain = 1.0
    for axis_at, parts in shards:
        draws = jax.random.uniform(jax.random.fold_in(jax.random.fold_in(key, 6), axis_at), (parts,), jnp.float32, least / len(shards), high / len(shards))
        gain = gain * jnp.repeat(jnp.exp(draws), shape[axis_at] // parts).reshape((-1,) + (1,) * (len(shape) - 1 - axis_at))
    return gain


def length_profile(count, total, reach, slope):
    weights = [(1 << 20) // math.isqrt(standing ** slope) + 1 for standing in range(2, count + 1)]
    spare, holding = total - reach - (count - 1), [1] * (count - 1)
    while spare > 0:
        free = [i for i in range(count - 1) if holding[i] < reach]
        whole, left = sum([weights[i] for i in free]), spare
        for i in free:
            more = min(reach - holding[i], max(1, left * weights[i] // whole), spare)
            holding[i] = holding[i] + more
            spare = spare - more
    return np.array([reach] + holding)


def ragged(key, amount, total, bound, skew):
    if amount == 2:
        one = jax.random.randint(key, (), max(1, total - bound), min(bound, total - 1) + 1)
        return jnp.stack([one, total - one])
    sizes = jnp.asarray(length_profile(amount, total, bound, skew), jnp.int32)
    twos = (amount - 1) // 2
    source_of, sink = sizes[1:1 + 2 * twos:2], sizes[2:2 + 2 * twos:2]
    margin = jnp.minimum(source_of - 1, bound - sink)
    passed = jax.random.randint(jax.random.fold_in(key, 1), (twos,), 0, 1 << 20) % (margin + 1)
    sizes = sizes.at[1:1 + 2 * twos:2].set(source_of - passed).at[2:2 + 2 * twos:2].set(sink + passed)
    return sizes[jax.random.permutation(jax.random.fold_in(key, 2), amount)]


def centred(rng, shape, scale, limit, shards=(), kind=jnp.bfloat16):
    values = jax.random.normal(rng, shape, jnp.float32) * scale
    if len(shards) > 0:
        values = steps_of(rng, shape, shards, -0.22, 0.18) * values
    return jnp.clip(values, min=-limit, max=limit).astype(kind)


def setup_inputs(seed: int = 0) -> dict:
    key_of = jax.random.split(jax.random.key(seed), 8)
    query_blocks = draw_query_blocks(jax.random.fold_in(key_of[7], 71), 0)
    key_blocks = draw_key_blocks(jax.random.fold_in(key_of[7], 71), 0)
    value_blocks = centred(key_of[2], (SAMPLES, LEN, HF), 1.0, 6.0, ((0, 8), (1, 32)))
    value_scales = jnp.clip(jnp.exp(math.log(4.0) - 2.7725887 * jax.random.uniform(key_of[3], (SAMPLES, LEN, HEADS), jnp.float32) ** steps_of(key_of[3], (SAMPLES, LEN, HEADS), ((0, 8), (1, 32)), -0.2, 0.2)), 0.25, 4.0)
    targets = draw_targets(jax.random.fold_in(key_of[7], 71), 0)
    frame_ids = jax.vmap(lambda own: jnp.searchsorted(jnp.cumsum(ragged(own, FRAMES, LEN, FRAME_MOST, 0)), jnp.arange(LEN), side="right"))(jax.random.split(key_of[5], SAMPLES)).reshape((SAMPLES, LEN)).astype(jnp.int32)
    bucket_ids = touch_ends(jax.random.randint(key_of[6], (SAMPLES,), 0, NB), jax.random.fold_in(key_of[6], 1), 0, NB - 1).astype(jnp.int32)
    return dict(query_blocks=query_blocks, key_blocks=key_blocks, value_blocks=value_blocks, value_scales=value_scales, targets=targets, frame_ids=frame_ids, bucket_ids=bucket_ids)


def rotate(values, frame_ids, direction_sign):
    quarter = values.shape[-1] // 4
    inverse_freq = 10000.0 ** (-jnp.arange(quarter, dtype=jnp.float32) / quarter)
    angles = frame_ids.astype(jnp.float32)[..., None] * inverse_freq
    cosine = jnp.cos(angles)[..., None, :]
    sine_part = direction_sign * jnp.sin(angles)[..., None, :]
    first_half = values[..., :quarter]
    second_half = values[..., quarter:2 * quarter]
    return jnp.concatenate([first_half * cosine - second_half * sine_part,
                            first_half * sine_part + second_half * cosine,
                            values[..., 2 * quarter:]], axis=-1)


def rounded(values):
    return lax.optimization_barrier(values.astype(jnp.bfloat16)).astype(jnp.float32)


def sample_grads(pieces):
    query_rows, key_rows, value_rows, scale_rows, target_rows, frame_rows = pieces
    length = query_rows.shape[0]
    shaped = (length, HEADS, HD)
    query_rot = rounded(rotate(query_rows.astype(jnp.float32).reshape(shaped), frame_rows, 1.0))
    key_rot = rounded(rotate(key_rows.astype(jnp.float32).reshape(shaped), frame_rows, 1.0))
    value_deq = rounded(value_rows.astype(jnp.float32).reshape(shaped) * scale_rows[:, :, None])
    score_scale = HD ** -0.5
    scores = jnp.einsum('qhd,khd->hqk', query_rot, key_rot) * score_scale
    row_max = jnp.max(scores, axis=-1, keepdims=True)
    exp_scores = jnp.exp(scores - row_max)
    row_total = jnp.sum(exp_scores, axis=-1, keepdims=True)
    probs_full = exp_scores / row_total
    probs_low = rounded(probs_full)
    attended = rounded(jnp.einsum('hqk,khd->qhd', probs_low, value_deq))
    errors = attended - target_rows.astype(jnp.float32).reshape(shaped)
    loss = jnp.mean(errors * errors)
    cotangent = rounded(errors)
    grad_value = jnp.einsum('hqk,qhd->khd', probs_low, cotangent)
    grad_probs = jnp.einsum('qhd,khd->hqk', cotangent, value_deq)
    row_delta = jnp.transpose(jnp.sum(cotangent * attended, axis=-1))[:, :, None]
    grad_scores = rounded(probs_full * (grad_probs - row_delta) * score_scale)
    grad_query = jnp.einsum('hqk,khd->qhd', grad_scores, key_rot)
    grad_key = jnp.einsum('hqk,qhd->khd', grad_scores, query_rot)
    return (grad_query.astype(jnp.bfloat16), grad_key.astype(jnp.bfloat16),
            grad_value.astype(jnp.bfloat16), loss)


def reference(query_blocks, key_blocks, value_blocks, value_scales, targets, frame_ids, bucket_ids):
    grad_query, grad_key, grad_value, loss = lax.map(
        sample_grads, (query_blocks, key_blocks, value_blocks, value_scales, targets, frame_ids))
    onehot = (bucket_ids[:, None] == jnp.arange(NB, dtype=jnp.int32)[None, :]).astype(jnp.float32)
    bucket_loss = jnp.sum(onehot * loss[:, None], axis=0)
    bucket_count = jnp.sum(onehot, axis=0)
    mean_all = jnp.sum(bucket_loss) / jnp.sum(bucket_count)
    chosen_loss = jnp.sum(onehot * bucket_loss[None, :], axis=1)
    chosen_count = jnp.sum(onehot * bucket_count[None, :], axis=1)
    weight = mean_all / (chosen_loss / chosen_count + 1e-5)
    scaled = weight[:, None, None, None]
    query_grad = (scaled * rotate(grad_query.astype(jnp.float32), frame_ids, -1.0)).astype(jnp.bfloat16)
    key_grad = (scaled * rotate(grad_key.astype(jnp.float32), frame_ids, -1.0)).astype(jnp.bfloat16)
    value_grad = (scaled * grad_value.astype(jnp.float32) * value_scales[..., None]).astype(jnp.bfloat16)
    full_shape = (SAMPLES, LEN, HEADS * HD)
    return query_grad.reshape(full_shape), key_grad.reshape(full_shape), value_grad.reshape(full_shape)
```

```python
import functools
import math

import jax
import jax.numpy as jnp
import numpy as np
from jax import lax
from jax.experimental import pallas as pl
from jax.experimental.pallas import tpu as pltpu
from jax.sharding import PartitionSpec as P

MESH = pl.DeviceIdType.MESH
HD = 128
LEN = 2048
NB = 8
QUARTER = HD // 4
ZS, YS = 8, 4
QB = 256
F32 = jnp.float32
BF16 = jnp.bfloat16


def kernel(
    n_dp,
    n_seq,
    q_ref,
    k_ref,
    v_ref,
    t_ref,
    scale_ref,
    frame_ref,
    freq_ref,
    bucket_ref,
    oq_ref,
    ok_ref,
    ov_ref,
    send_in,
    recv_in,
    send_g,
    recv_g,
    grad_k,
    grad_v,
    loss_acc,
    loss_mine,
    loss_dp,
    loss_plane,
    loss_seq,
    in_send,
    in_recv,
    g_send,
    g_recv,
    dp_send,
    dp_recv,
    seq_send,
    seq_recv,
    own_sem,
):
    samples, rows, width = q_ref.shape
    dp = lax.axis_index("dp")
    me = lax.axis_index("seq")
    my_z, my_y = me // YS, me % YS

    def partner(i):
        a, dy = i // YS, i % YS
        half = (a + 1) // 2
        dz = half * (1 - 2 * (a % 2)) + ZS
        return ((my_z + dz) % ZS) * YS + (my_y + dy) % YS

    barrier = pltpu.get_barrier_semaphore()

    @pl.loop(1, n_seq)
    def _(i):
        pl.semaphore_signal(barrier, inc=1, device_id=(dp, (me + i) % n_seq), device_id_type=MESH)

    @pl.loop(1, n_dp)
    def _(i):
        pl.semaphore_signal(barrier, inc=1, device_id=((dp + i) % n_dp, me), device_id_type=MESH)

    pl.semaphore_wait(barrier, n_seq + n_dp - 2)

    lane = lax.broadcasted_iota(jnp.int32, (1, HD), 1)

    def tables(s):
        eye = lax.broadcasted_iota(jnp.int32, (rows, rows), 0) == lax.broadcasted_iota(
            jnp.int32, (rows, rows), 1
        )
        ids = frame_ref[s : s + 1, :].astype(F32)
        column = jnp.sum(jnp.where(eye, ids, 0.0), axis=1, keepdims=True)
        angle = column * freq_ref[...]
        cosine = jnp.where(lane < 2 * QUARTER, jnp.cos(angle), 1.0)
        sine = jnp.sin(angle)
        low = jnp.where(lane < QUARTER, -sine, 0.0)
        high = jnp.where((lane >= QUARTER) & (lane < 2 * QUARTER), sine, 0.0)
        return cosine, low, high

    def turn(x, cosine, low, high):
        return (
            x * cosine
            + pltpu.roll(x, HD - QUARTER, 1) * low
            + pltpu.roll(x, QUARTER, 1) * high
        )

    def in_copy(s, i):
        to = partner(i)
        return pltpu.make_async_remote_copy(
            src_ref=send_in.at[s, to],
            dst_ref=recv_in.at[s, :, pl.ds(pl.multiple_of(me * rows, rows), rows), :],
            send_sem=in_send.at[s, i],
            recv_sem=in_recv.at[s, me],
            device_id=(dp, to),
            device_id_type=MESH,
        )

    def in_own(s):
        return pltpu.make_async_copy(
            send_in.at[s, me],
            recv_in.at[s, :, pl.ds(pl.multiple_of(me * rows, rows), rows), :],
            own_sem.at[0, s],
        )

    def wait_in(s):
        @pl.loop(1, n_seq)
        def _(i):
            src = (me + i) % n_seq
            pltpu.make_async_remote_copy(
                src_ref=send_in.at[s, src],
                dst_ref=recv_in.at[s, :, pl.ds(pl.multiple_of(src * rows, rows), rows), :],
                send_sem=in_send.at[s, i],
                recv_sem=in_recv.at[s, src],
                device_id=(dp, src),
                device_id_type=MESH,
            ).wait_recv()

        in_own(s).wait()

    def g_copy(s, i):
        to = partner(i)
        return pltpu.make_async_remote_copy(
            src_ref=send_g.at[s, :, pl.ds(pl.multiple_of(to * rows, rows), rows), :],
            dst_ref=recv_g.at[s, me],
            send_sem=g_send.at[s, i],
            recv_sem=g_recv.at[s, me],
            device_id=(dp, to),
            device_id_type=MESH,
        )

    def g_own(s):
        return pltpu.make_async_copy(
            send_g.at[s, :, pl.ds(pl.multiple_of(me * rows, rows), rows), :],
            recv_g.at[s, me],
            own_sem.at[1, s],
        )

    def prepare(s):
        turns = tables(s)
        scales = scale_ref[s]
        head_lane = lax.broadcasted_iota(jnp.int32, scales.shape, 1)

        def fill(head):
            columns = pl.ds(pl.multiple_of(head * HD, HD), HD)
            send_in[s, head, 0] = turn(q_ref[s, :, columns].astype(F32), *turns).astype(BF16)
            send_in[s, head, 1] = turn(k_ref[s, :, columns].astype(F32), *turns).astype(BF16)
            scale = jnp.sum(jnp.where(head_lane == head, scales, 0.0), axis=1, keepdims=True)
            send_in[s, head, 2] = (v_ref[s, :, columns].astype(F32) * scale).astype(BF16)
            send_in[s, head, 3] = t_ref[s, :, columns]

        @pl.loop(1, n_seq)
        def _(j):
            i = n_seq - j
            fill(partner(i))
            if s > 0:
                in_copy(s - 1, i).wait_send()
            in_copy(s, i).start()

        fill(me)
        in_own(s).start()

    def attend(s):
        grad_k[...] = jnp.zeros_like(grad_k)
        grad_v[...] = jnp.zeros_like(grad_v)
        loss_acc[s] = jnp.zeros_like(loss_acc[s])

        @pl.loop(0, LEN // QB)
        def _(b):
            block = pl.ds(pl.multiple_of(b * QB, QB), QB)
            q = recv_in[s, 0, block]
            k = recv_in[s, 1]
            v = recv_in[s, 2]
            scores = lax.dot_general(q, k, (((1,), (1,)), ((), ())), preferred_element_type=F32)
            top = jnp.max(scores, axis=1, keepdims=True)
            e = jnp.exp2((scores - top) * (HD**-0.5 * math.log2(math.e)))
            p = e * (1.0 / jnp.sum(e, axis=1, keepdims=True))
            p_low = p.astype(BF16)
            attended = jnp.dot(p_low, v, preferred_element_type=F32).astype(BF16).astype(F32)
            errors = attended - recv_in[s, 3, block].astype(F32)
            loss_acc[s] += jnp.sum((errors * errors).reshape(QB // 8, 8, HD), axis=0)
            cotangent = errors.astype(BF16)
            delta = jnp.sum(cotangent.astype(F32) * attended, axis=1, keepdims=True)
            grad_v[...] += lax.dot_general(
                p_low, cotangent, (((0,), (0,)), ((), ())), preferred_element_type=F32
            )
            grad_p = lax.dot_general(
                cotangent, v, (((1,), (1,)), ((), ())), preferred_element_type=F32
            )
            grad_s = (p * (grad_p - delta) * HD**-0.5).astype(BF16)
            send_g[s, 0, block] = jnp.dot(grad_s, k, preferred_element_type=F32).astype(BF16)
            grad_k[...] += lax.dot_general(
                grad_s, q, (((0,), (0,)), ((), ())), preferred_element_type=F32
            )

        send_g[s, 1] = grad_k[...].astype(BF16)
        send_g[s, 2] = grad_v[...].astype(BF16)

    def start_g(s):
        @pl.loop(1, n_seq)
        def _(j):
            g_copy(s, n_seq - j).start()

        g_own(s).start()

    for s in range(samples):
        prepare(s)
    for s in range(samples):
        wait_in(s)
        attend(s)
        if s == 0:
            @pl.loop(1, n_seq)
            def _(i):
                in_copy(samples - 1, i).wait_send()

        if s < samples - 1:
            start_g(s)

    mine = jnp.zeros((8, HD), F32)
    for s in range(samples):
        bucket = bucket_ref[s]
        total = jnp.sum(jnp.sum(loss_acc[s], axis=0, keepdims=True), axis=1, keepdims=True)
        mine += jnp.where(lane == bucket, total / (LEN * width), 0.0)
        mine += jnp.where(lane == bucket + NB, 1.0 / n_seq, 0.0)
    loss_mine[...] = mine

    def dp_copy(i):
        to = (dp + i) % n_dp
        return pltpu.make_async_remote_copy(
            src_ref=loss_mine,
            dst_ref=loss_dp.at[dp],
            send_sem=dp_send.at[i],
            recv_sem=dp_recv.at[dp],
            device_id=(to, me),
            device_id_type=MESH,
        )

    def seq_copy(i):
        to = (me + i) % n_seq
        return pltpu.make_async_remote_copy(
            src_ref=loss_plane,
            dst_ref=loss_seq.at[me],
            send_sem=seq_send.at[i],
            recv_sem=seq_recv.at[me],
            device_id=(dp, to),
            device_id_type=MESH,
        )

    @pl.loop(1, n_dp)
    def _(i):
        dp_copy(i).start()

    loss_dp[dp] = mine

    @pl.loop(1, n_dp)
    def _(i):
        src = (dp + i) % n_dp
        pltpu.make_async_remote_copy(
            src_ref=loss_mine,
            dst_ref=loss_dp.at[src],
            send_sem=dp_send.at[i],
            recv_sem=dp_recv.at[src],
            device_id=(src, me),
            device_id_type=MESH,
        ).wait_recv()

    plane = jnp.sum(loss_dp[...], axis=0)
    loss_plane[...] = plane

    @pl.loop(1, n_seq)
    def _(i):
        seq_copy(i).start()

    loss_seq[me] = plane
    start_g(samples - 1)

    @pl.loop(1, n_seq)
    def _(i):
        src = (me + i) % n_seq
        pltpu.make_async_remote_copy(
            src_ref=loss_plane,
            dst_ref=loss_seq.at[src],
            send_sem=seq_send.at[i],
            recv_sem=seq_recv.at[src],
            device_id=(dp, src),
            device_id_type=MESH,
        ).wait_recv()

    buckets = jnp.sum(loss_seq[...], axis=0)[0:1, :]
    sum_loss = jnp.sum(jnp.where(lane < NB, buckets, 0.0), axis=1, keepdims=True)
    sum_count = jnp.sum(
        jnp.where((lane >= NB) & (lane < 2 * NB), buckets, 0.0), axis=1, keepdims=True
    )
    mean_all = sum_loss / sum_count

    for s in range(samples):
        bucket = bucket_ref[s]
        chosen_loss = jnp.sum(jnp.where(lane == bucket, buckets, 0.0), axis=1, keepdims=True)
        chosen_count = jnp.sum(
            jnp.where(lane == bucket + NB, buckets, 0.0), axis=1, keepdims=True
        )
        weight = mean_all / (chosen_loss / chosen_count + 1e-5)
        cosine, low, high = tables(s)
        scales = scale_ref[s]
        head_lane = lax.broadcasted_iota(jnp.int32, scales.shape, 1)

        def finish(head):
            columns = pl.ds(pl.multiple_of(head * HD, HD), HD)
            for array, out in ((0, oq_ref), (1, ok_ref)):
                turned = turn(recv_g[s, head, array].astype(F32), cosine, -low, -high)
                out[s, :, columns] = (weight * turned).astype(BF16)
            scale = jnp.sum(jnp.where(head_lane == head, scales, 0.0), axis=1, keepdims=True)
            ov_ref[s, :, columns] = (weight * recv_g[s, head, 2].astype(F32) * scale).astype(BF16)

        g_own(s).wait()
        finish(me)

        @pl.loop(1, n_seq)
        def _(j):
            i = n_seq - j
            src = (me + i) % n_seq
            pltpu.make_async_remote_copy(
                src_ref=send_g.at[s, :, pl.ds(pl.multiple_of(src * rows, rows), rows), :],
                dst_ref=recv_g.at[s, src],
                send_sem=g_send.at[s, i],
                recv_sem=g_recv.at[s, src],
                device_id=(dp, src),
                device_id_type=MESH,
            ).wait_recv()
            finish(src)

    @pl.loop(1, n_seq)
    def _(i):
        for s in range(samples):
            g_copy(s, i).wait_send()
        seq_copy(i).wait_send()

    @pl.loop(1, n_dp)
    def _(i):
        dp_copy(i).wait_send()


def local(n_dp, n_seq, q, k, v, scales, targets, frame_ids, bucket_ids):
    samples, rows, width = q.shape
    exponent = np.arange(HD) % QUARTER / QUARTER
    freq = np.where(np.arange(HD) < 2 * QUARTER, 10000.0 ** (-exponent), 0.0)
    freq = jnp.asarray(freq[None, :], F32)
    out = jax.ShapeDtypeStruct(q.shape, BF16)
    vmem = pl.BlockSpec(memory_space=pltpu.VMEM)
    dma = pltpu.SemaphoreType.DMA
    return tuple(
        pl.pallas_call(
            functools.partial(kernel, n_dp, n_seq),
            out_shape=(out, out, out),
            in_specs=[vmem] * 7 + [pl.BlockSpec(memory_space=pltpu.SMEM)],
            out_specs=(vmem, vmem, vmem),
            scratch_shapes=[
                pltpu.VMEM((samples, n_seq, 4, rows, HD), BF16),
                pltpu.VMEM((samples, 4, LEN, HD), BF16),
                pltpu.VMEM((samples, 3, LEN, HD), BF16),
                pltpu.VMEM((samples, n_seq, 3, rows, HD), BF16),
                pltpu.VMEM((LEN, HD), F32),
                pltpu.VMEM((LEN, HD), F32),
                pltpu.VMEM((samples, 8, HD), F32),
                pltpu.VMEM((8, HD), F32),
                pltpu.VMEM((n_dp, 8, HD), F32),
                pltpu.VMEM((8, HD), F32),
                pltpu.VMEM((n_seq, 8, HD), F32),
                dma((samples, n_seq)),
                dma((samples, n_seq)),
                dma((samples, n_seq)),
                dma((samples, n_seq)),
                dma((n_dp,)),
                dma((n_dp,)),
                dma((n_seq,)),
                dma((n_seq,)),
                dma((2, samples)),
            ],
            compiler_params=pltpu.CompilerParams(
                collective_id=0, has_side_effects=True, vmem_limit_bytes=58 << 20
            ),
        )(q, k, v, targets, scales, frame_ids, freq, bucket_ids)
    )


def solution(mesh):
    spec = P("dp", "seq", None)
    return jax.shard_map(
        functools.partial(local, mesh.shape["dp"], mesh.shape["seq"]),
        mesh=mesh,
        in_specs=(spec, spec, spec, spec, spec, P("dp", "seq"), P("dp")),
        out_specs=(spec, spec, spec),
        check_vma=False,
    )
```

```python
import functools
import math

import jax
import jax.numpy as jnp
import numpy as np
from jax import lax
from jax.experimental import pallas as pl
from jax.experimental.pallas import tpu as pltpu
from jax.sharding import PartitionSpec as P

MESH = pl.DeviceIdType.MESH
HD = 128
LEN = 2048
NB = 8
QUARTER = HD // 4
ZS, YS = 8, 4
QB = 256
F32 = jnp.float32
BF16 = jnp.bfloat16


def turn(x, cosine, low, high):
    return (
        x * cosine + pltpu.roll(x, HD - QUARTER, 1) * low + pltpu.roll(x, QUARTER, 1) * high
    )


def kernel(
    n_dp,
    n_seq,
    q_ref,
    k_ref,
    v_ref,
    t_ref,
    scale_ref,
    frame_ref,
    freq_ref,
    bucket_ref,
    recv_g,
    turn_ref,
    weighed_ref,
    held,
    send_in,
    recv_in,
    send_g,
    grad_k,
    grad_v,
    loss_acc,
    loss_mine,
    loss_dp,
    loss_plane,
    loss_seq,
    in_send,
    in_recv,
    g_send,
    g_recv,
    dp_send,
    dp_recv,
    seq_send,
    seq_recv,
    own_sem,
    load_sem,
):
    samples, rows, width = q_ref.shape
    last = samples - 1
    dp = lax.axis_index("dp")
    me = lax.axis_index("seq")
    my_z, my_y = me // YS, me % YS

    def partner(i):
        a, dy = i // YS, i % YS
        half = (a + 1) // 2
        dz = half * (1 - 2 * (a % 2)) + ZS
        return ((my_z + dz) % ZS) * YS + (my_y + dy) % YS

    barrier = pltpu.get_barrier_semaphore()

    @pl.loop(1, n_seq)
    def _(i):
        pl.semaphore_signal(barrier, inc=1, device_id=(dp, (me + i) % n_seq), device_id_type=MESH)

    @pl.loop(1, n_dp)
    def _(i):
        pl.semaphore_signal(barrier, inc=1, device_id=((dp + i) % n_dp, me), device_id_type=MESH)

    def load(s, array):
        source = (q_ref, k_ref, v_ref, t_ref)[array]
        return pltpu.make_async_copy(source.at[s], held.at[s, array], load_sem.at[s, array])

    for s in range(samples):
        for array in range(4):
            load(s, array).start()

    lane = lax.broadcasted_iota(jnp.int32, (1, HD), 1)

    def upright(row):
        eye = lax.broadcasted_iota(jnp.int32, (rows, rows), 0) == lax.broadcasted_iota(
            jnp.int32, (rows, rows), 1
        )
        return jnp.sum(jnp.where(eye, row, 0.0), axis=1, keepdims=True)

    def tables(s):
        angle = upright(frame_ref[s : s + 1, :].astype(F32)) * freq_ref[...]
        cosine = jnp.where(lane < 2 * QUARTER, jnp.cos(angle), 1.0)
        sine = jnp.sin(angle)
        low = jnp.where(lane < QUARTER, -sine, 0.0)
        high = jnp.where((lane >= QUARTER) & (lane < 2 * QUARTER), sine, 0.0)
        return cosine, low, high

    def in_copy(s, i):
        to = partner(i)
        return pltpu.make_async_remote_copy(
            src_ref=send_in.at[s, to],
            dst_ref=recv_in.at[s, :, pl.ds(pl.multiple_of(me * rows, rows), rows), :],
            send_sem=in_send.at[s, i],
            recv_sem=in_recv.at[s, me],
            device_id=(dp, to),
            device_id_type=MESH,
        )

    def in_own(s):
        return pltpu.make_async_copy(
            send_in.at[s, me],
            recv_in.at[s, :, pl.ds(pl.multiple_of(me * rows, rows), rows), :],
            own_sem.at[0, s],
        )

    def wait_in(s):
        @pl.loop(1, n_seq)
        def _(i):
            src = (me + i) % n_seq
            pltpu.make_async_remote_copy(
                src_ref=send_in.at[s, src],
                dst_ref=recv_in.at[s, :, pl.ds(pl.multiple_of(src * rows, rows), rows), :],
                send_sem=in_send.at[s, i],
                recv_sem=in_recv.at[s, src],
                device_id=(dp, src),
                device_id_type=MESH,
            ).wait_recv()

        in_own(s).wait()

    def g_copy(s, i):
        to = partner(i)
        return pltpu.make_async_remote_copy(
            src_ref=send_g.at[s, :, pl.ds(pl.multiple_of(to * rows, rows), rows), :],
            dst_ref=recv_g.at[s, me],
            send_sem=g_send.at[s, i],
            recv_sem=g_recv.at[s, me],
            device_id=(dp, to),
            device_id_type=MESH,
        )

    def g_own(s):
        return pltpu.make_async_copy(
            send_g.at[s, :, pl.ds(pl.multiple_of(me * rows, rows), rows), :],
            recv_g.at[s, me],
            own_sem.at[1, s],
        )

    def prepare(s):
        turns = tables(s)
        for array in range(4):
            load(s, array).wait()

        @pl.loop(0, n_seq)
        def _(head):
            columns = pl.ds(pl.multiple_of(head * HD, HD), HD)
            send_in[s, head, 0] = turn(held[s, 0, :, columns].astype(F32), *turns).astype(BF16)
            send_in[s, head, 1] = turn(held[s, 1, :, columns].astype(F32), *turns).astype(BF16)
            scale = upright(scale_ref[s, pl.ds(head, 1), :])
            send_in[s, head, 2] = (held[s, 2, :, columns].astype(F32) * scale).astype(BF16)
            send_in[s, head, 3] = held[s, 3, :, columns]

    def attend(s):
        grad_k[...] = jnp.zeros_like(grad_k)
        grad_v[...] = jnp.zeros_like(grad_v)
        loss_acc[s] = jnp.zeros_like(loss_acc[s])

        @pl.loop(0, LEN // QB)
        def _(b):
            block = pl.ds(pl.multiple_of(b * QB, QB), QB)
            q = recv_in[s, 0, block]
            k = recv_in[s, 1]
            v = recv_in[s, 2]
            scores = lax.dot_general(q, k, (((1,), (1,)), ((), ())), preferred_element_type=F32)
            top = jnp.max(scores, axis=1, keepdims=True)
            e = jnp.exp2((scores - top) * (HD**-0.5 * math.log2(math.e)))
            p = e * (1.0 / jnp.sum(e, axis=1, keepdims=True))
            p_low = p.astype(BF16)
            attended = jnp.dot(p_low, v, preferred_element_type=F32).astype(BF16).astype(F32)
            errors = attended - recv_in[s, 3, block].astype(F32)
            loss_acc[s] += jnp.sum((errors * errors).reshape(QB // 8, 8, HD), axis=0)
            cotangent = errors.astype(BF16)
            delta = jnp.sum(cotangent.astype(F32) * attended, axis=1, keepdims=True)
            grad_v[...] += lax.dot_general(
                p_low, cotangent, (((0,), (0,)), ((), ())), preferred_element_type=F32
            )
            grad_p = lax.dot_general(
                cotangent, v, (((1,), (1,)), ((), ())), preferred_element_type=F32
            )
            grad_s = (p * (grad_p - delta) * HD**-0.5).astype(BF16)
            send_g[s, 0, block] = jnp.dot(grad_s, k, preferred_element_type=F32).astype(BF16)
            grad_k[...] += lax.dot_general(
                grad_s, q, (((0,), (0,)), ((), ())), preferred_element_type=F32
            )

        send_g[s, 1] = grad_k[...].astype(BF16)
        send_g[s, 2] = grad_v[...].astype(BF16)

    def start_in(s):
        @pl.loop(1, n_seq)
        def _(j):
            i = n_seq - j
            if s > 0:
                in_copy(s - 1, i).wait_send()
            in_copy(s, i).start()

        in_own(s).start()

    def start_g(s):
        @pl.loop(1, n_seq)
        def _(j):
            g_copy(s, n_seq - j).start()

        g_own(s).start()

    prepare(0)
    pl.semaphore_wait(barrier, n_seq + n_dp - 2)
    start_in(0)
    for s in range(1, samples):
        prepare(s)
        start_in(s)

    @pl.loop(0, samples)
    def _(s):
        wait_in(s)
        attend(s)

        @pl.when(s == 0)
        def _():
            @pl.loop(1, n_seq)
            def _(i):
                in_copy(last, i).wait_send()

        start_g(s)

    mine = jnp.zeros((8, HD), F32)
    for s in range(samples):
        bucket = bucket_ref[s]
        total = jnp.sum(jnp.sum(loss_acc[s], axis=0, keepdims=True), axis=1, keepdims=True)
        mine += jnp.where(lane == bucket, total / (LEN * width), 0.0)
        mine += jnp.where(lane == bucket + NB, 1.0 / n_seq, 0.0)
    loss_mine[...] = mine

    def dp_copy(i):
        to = (dp + i) % n_dp
        return pltpu.make_async_remote_copy(
            src_ref=loss_mine,
            dst_ref=loss_dp.at[dp],
            send_sem=dp_send.at[i],
            recv_sem=dp_recv.at[dp],
            device_id=(to, me),
            device_id_type=MESH,
        )

    def seq_copy(i):
        to = (me + i) % n_seq
        return pltpu.make_async_remote_copy(
            src_ref=loss_plane,
            dst_ref=loss_seq.at[me],
            send_sem=seq_send.at[i],
            recv_sem=seq_recv.at[me],
            device_id=(dp, to),
            device_id_type=MESH,
        )

    @pl.loop(1, n_dp)
    def _(i):
        dp_copy(i).start()

    loss_dp[dp] = mine

    @pl.loop(1, n_dp)
    def _(i):
        src = (dp + i) % n_dp
        pltpu.make_async_remote_copy(
            src_ref=loss_mine,
            dst_ref=loss_dp.at[src],
            send_sem=dp_send.at[i],
            recv_sem=dp_recv.at[src],
            device_id=(src, me),
            device_id_type=MESH,
        ).wait_recv()

    plane = jnp.sum(loss_dp[...], axis=0)
    loss_plane[...] = plane

    @pl.loop(1, n_seq)
    def _(i):
        seq_copy(i).start()

    loss_seq[me] = plane

    @pl.loop(1, n_seq)
    def _(i):
        src = (me + i) % n_seq
        pltpu.make_async_remote_copy(
            src_ref=loss_plane,
            dst_ref=loss_seq.at[src],
            send_sem=seq_send.at[i],
            recv_sem=seq_recv.at[src],
            device_id=(dp, src),
            device_id_type=MESH,
        ).wait_recv()

    buckets = jnp.sum(loss_seq[...], axis=0)[0:1, :]
    sum_loss = jnp.sum(jnp.where(lane < NB, buckets, 0.0), axis=1, keepdims=True)
    sum_count = jnp.sum(
        jnp.where((lane >= NB) & (lane < 2 * NB), buckets, 0.0), axis=1, keepdims=True
    )
    mean_all = sum_loss / sum_count

    for s in range(samples):
        bucket = bucket_ref[s]
        chosen_loss = jnp.sum(jnp.where(lane == bucket, buckets, 0.0), axis=1, keepdims=True)
        chosen_count = jnp.sum(
            jnp.where(lane == bucket + NB, buckets, 0.0), axis=1, keepdims=True
        )
        weight = mean_all / (chosen_loss / chosen_count + 1e-5)
        cosine, low, high = tables(s)
        turn_ref[s, 0] = weight * cosine
        turn_ref[s, 1] = -weight * low
        turn_ref[s, 2] = -weight * high
        weighed_ref[s] = weight * scale_ref[s]

    for s in range(samples):
        g_own(s).wait()

        @pl.loop(1, n_seq)
        def _(i):
            src = (me + i) % n_seq
            pltpu.make_async_remote_copy(
                src_ref=send_g.at[s, :, pl.ds(pl.multiple_of(src * rows, rows), rows), :],
                dst_ref=recv_g.at[s, src],
                send_sem=g_send.at[s, i],
                recv_sem=g_recv.at[s, src],
                device_id=(dp, src),
                device_id_type=MESH,
            ).wait_recv()

    @pl.loop(1, n_seq)
    def _(i):
        for s in range(samples):
            g_copy(s, i).wait_send()
        seq_copy(i).wait_send()

    @pl.loop(1, n_dp)
    def _(i):
        dp_copy(i).wait_send()


def finish(heads, grad_ref, turn_ref, weighed_ref, oq_ref, ok_ref, ov_ref):
    rows = grad_ref.shape[3]
    cosine, low, high = turn_ref[0, 0], turn_ref[0, 1], turn_ref[0, 2]
    eye = lax.broadcasted_iota(jnp.int32, (rows, rows), 0) == lax.broadcasted_iota(
        jnp.int32, (rows, rows), 1
    )
    first = pl.program_id(1) * heads
    for h in range(heads):
        columns = slice(h * HD, (h + 1) * HD)
        oq_ref[0, :, columns] = turn(grad_ref[0, h, 0].astype(F32), cosine, low, high).astype(BF16)
        ok_ref[0, :, columns] = turn(grad_ref[0, h, 1].astype(F32), cosine, low, high).astype(BF16)
        row = weighed_ref[0, pl.ds(first + h, 1), :]
        scale = jnp.sum(jnp.where(eye, row, 0.0), axis=1, keepdims=True)
        ov_ref[0, :, columns] = (grad_ref[0, h, 2].astype(F32) * scale).astype(BF16)


def local(n_dp, n_seq, q, k, v, scales, targets, frame_ids, bucket_ids):
    samples, rows, width = q.shape
    exponent = np.arange(HD) % QUARTER / QUARTER
    freq = np.where(np.arange(HD) < 2 * QUARTER, 10000.0 ** (-exponent), 0.0)
    freq = jnp.asarray(freq[None, :], F32)
    scales = jnp.swapaxes(scales, 1, 2)
    vmem = pl.BlockSpec(memory_space=pltpu.VMEM)
    smem = pl.BlockSpec(memory_space=pltpu.SMEM)
    anywhere = pl.BlockSpec(memory_space=pl.ANY)
    dma = pltpu.SemaphoreType.DMA
    grads, turns, weighed = pl.pallas_call(
        functools.partial(kernel, n_dp, n_seq),
        out_shape=(
            jax.ShapeDtypeStruct((samples, n_seq, 3, rows, HD), BF16),
            jax.ShapeDtypeStruct((samples, 3, rows, HD), F32),
            jax.ShapeDtypeStruct(scales.shape, F32),
        ),
        in_specs=[anywhere] * 4 + [vmem] * 3 + [smem],
        out_specs=(anywhere, vmem, vmem),
        scratch_shapes=[
            pltpu.VMEM((samples, 4, rows, width), BF16),
            pltpu.VMEM((samples, n_seq, 4, rows, HD), BF16),
            pltpu.VMEM((samples, 4, LEN, HD), BF16),
            pltpu.VMEM((samples, 3, LEN, HD), BF16),
            pltpu.VMEM((LEN, HD), F32),
            pltpu.VMEM((LEN, HD), F32),
            pltpu.VMEM((samples, 8, HD), F32),
            pltpu.VMEM((8, HD), F32),
            pltpu.VMEM((n_dp, 8, HD), F32),
            pltpu.VMEM((8, HD), F32),
            pltpu.VMEM((n_seq, 8, HD), F32),
            dma((samples, n_seq)),
            dma((samples, n_seq)),
            dma((samples, n_seq)),
            dma((samples, n_seq)),
            dma((n_dp,)),
            dma((n_dp,)),
            dma((n_seq,)),
            dma((n_seq,)),
            dma((2, samples)),
            dma((samples, 4)),
        ],
        compiler_params=pltpu.CompilerParams(
            collective_id=0, has_side_effects=True, vmem_limit_bytes=58 << 20
        ),
    )(q, k, v, targets, scales, frame_ids, freq, bucket_ids)
    heads = 8
    out = jax.ShapeDtypeStruct(q.shape, BF16)
    out_spec = pl.BlockSpec((1, rows, heads * HD), lambda s, g: (s, 0, g))
    return tuple(
        pl.pallas_call(
            functools.partial(finish, heads),
            grid=(samples, n_seq // heads),
            out_shape=(out, out, out),
            in_specs=[
                pl.BlockSpec((1, heads, 3, rows, HD), lambda s, g: (s, g, 0, 0, 0)),
                pl.BlockSpec((1, 3, rows, HD), lambda s, g: (s, 0, 0, 0)),
                pl.BlockSpec((1, n_seq, rows), lambda s, g: (s, 0, 0)),
            ],
            out_specs=(out_spec, out_spec, out_spec),
            compiler_params=pltpu.CompilerParams(vmem_limit_bytes=58 << 20),
        )(grads, turns, weighed)
    )


def solution(mesh):
    spec = P("dp", "seq", None)
    return jax.shard_map(
        functools.partial(local, mesh.shape["dp"], mesh.shape["seq"]),
        mesh=mesh,
        in_specs=(spec, spec, spec, spec, spec, P("dp", "seq"), P("dp")),
        out_specs=(spec, spec, spec),
        check_vma=False,
    )
```

```python
import functools
import math

import jax
import jax.numpy as jnp
import numpy as np
from jax import lax
from jax.experimental import pallas as pl
from jax.experimental.pallas import tpu as pltpu
from jax.sharding import PartitionSpec as P

MESH = pl.DeviceIdType.MESH
HD = 128
LEN = 2048
NB = 8
QUARTER = HD // 4
ZS, YS = 8, 4
QB = 256
F32 = jnp.float32
BF16 = jnp.bfloat16


def swap_matrix():
    i = lax.broadcasted_iota(jnp.int32, (HD, HD), 0)
    j = lax.broadcasted_iota(jnp.int32, (HD, HD), 1)
    first = (j < QUARTER) & (i == j + QUARTER)
    second = (j >= QUARTER) & (j < 2 * QUARTER) & (i == j - QUARTER)
    return jnp.where(first | second, 1.0, 0.0).astype(BF16)


def turn(blocks, cosine, sine):
    x = jnp.concatenate(blocks, axis=0)
    swapped = jnp.dot(x, swap_matrix(), preferred_element_type=F32)
    shape = (len(blocks),) + blocks[0].shape
    turned = x.astype(F32).reshape(shape) * cosine + swapped.reshape(shape) * sine
    return turned.astype(BF16)


def kernel(
    n_dp,
    n_seq,
    q_ref,
    k_ref,
    v_ref,
    t_ref,
    scale_hbm,
    frame_hbm,
    freq_hbm,
    bucket_ref,
    recv_g,
    turn_hbm,
    weighed_hbm,
    scale_ref,
    frame_ref,
    freq_ref,
    turn_ref,
    weighed_ref,
    held,
    tables,
    upright,
    planes,
    send_in,
    recv_in,
    send_g,
    grad_k,
    grad_v,
    loss_acc,
    loss_mine,
    loss_dp,
    loss_plane,
    loss_seq,
    in_send,
    in_recv,
    t_send,
    t_recv,
    g_send,
    g_recv,
    dp_send,
    dp_recv,
    seq_send,
    seq_recv,
    own_sem,
    load_sem,
    side_sem,
):
    samples, rows, width = q_ref.shape
    last = samples - 1
    dp = lax.axis_index("dp")
    me = lax.axis_index("seq")
    my_z, my_y = me // YS, me % YS

    def partner(i):
        a, dy = i // YS, i % YS
        half = (a + 1) // 2
        dz = half * (1 - 2 * (a % 2)) + ZS
        return ((my_z + dz) % ZS) * YS + (my_y + dy) % YS

    barrier = pltpu.get_barrier_semaphore()

    @pl.loop(1, n_seq)
    def _(i):
        pl.semaphore_signal(barrier, inc=1, device_id=(dp, (me + i) % n_seq), device_id_type=MESH)

    @pl.loop(1, n_dp)
    def _(i):
        pl.semaphore_signal(barrier, inc=1, device_id=((dp + i) % n_dp, me), device_id_type=MESH)

    side = [
        pltpu.make_async_copy(source, there, side_sem.at[i])
        for i, (source, there) in enumerate(
            ((scale_hbm, scale_ref), (frame_hbm, frame_ref), (freq_hbm, freq_ref))
        )
    ]

    def load(s, array):
        source = (q_ref, k_ref, v_ref)[array]
        return pltpu.make_async_copy(source.at[s], held.at[s, array], load_sem.at[s, array])

    for copy in side:
        copy.start()
    for s in range(samples):
        for array in range(3):
            load(s, array).start()

    lane = lax.broadcasted_iota(jnp.int32, (1, HD), 1)
    eye = lax.broadcasted_iota(jnp.int32, (rows, rows), 0) == lax.broadcasted_iota(
        jnp.int32, (rows, rows), 1
    )

    def ready_tables(s):
        ids = frame_ref[s : s + 1, :].astype(F32)
        angle = jnp.sum(jnp.where(eye, ids, 0.0), axis=1, keepdims=True) * freq_ref[...]
        tables[s, 0] = jnp.where(lane < 2 * QUARTER, jnp.cos(angle), 1.0)
        sine = jnp.sin(angle)
        tables[s, 1] = jnp.where(
            lane < QUARTER, -sine, jnp.where(lane < 2 * QUARTER, sine, 0.0)
        )
        columns = jnp.transpose(scale_ref[s])
        upright[s] = columns
        for z in range(ZS):
            planes[s, z] = columns[:, z * YS : (z + 1) * YS]

    def rows_of(device):
        return pl.ds(pl.multiple_of(device * rows, rows), rows)

    def head_of(device):
        return pl.ds(pl.multiple_of(device * HD, HD), HD)

    def in_copy(s, to, source):
        return pltpu.make_async_remote_copy(
            src_ref=send_in.at[s, to],
            dst_ref=recv_in.at[s, pl.ds(0, 3), rows_of(source), :],
            send_sem=in_send.at[s, to],
            recv_sem=in_recv.at[s, source],
            device_id=(dp, to),
            device_id_type=MESH,
        )

    def t_copy(s, to, source):
        return pltpu.make_async_remote_copy(
            src_ref=t_ref.at[s, :, head_of(to)],
            dst_ref=recv_in.at[s, 3, rows_of(source), :],
            send_sem=t_send.at[s, to],
            recv_sem=t_recv.at[s, source],
            device_id=(dp, to),
            device_id_type=MESH,
        )

    def in_own(s):
        return pltpu.make_async_copy(
            send_in.at[s, me], recv_in.at[s, pl.ds(0, 3), rows_of(me), :], own_sem.at[0, s]
        )

    def t_own(s):
        return pltpu.make_async_copy(
            t_ref.at[s, :, head_of(me)], recv_in.at[s, 3, rows_of(me), :], own_sem.at[2, s]
        )

    def wait_in(s):
        @pl.loop(1, n_seq)
        def _(i):
            source = (me + i) % n_seq
            t_copy(s, source, source).wait_recv()
            in_copy(s, source, source).wait_recv()

        in_own(s).wait()
        t_own(s).wait()

    def g_copy(s, i):
        to = partner(i)
        return pltpu.make_async_remote_copy(
            src_ref=send_g.at[s, :, pl.ds(pl.multiple_of(to * rows, rows), rows), :],
            dst_ref=recv_g.at[s, me],
            send_sem=g_send.at[s, i],
            recv_sem=g_recv.at[s, me],
            device_id=(dp, to),
            device_id_type=MESH,
        )

    def g_own(s):
        return pltpu.make_async_copy(
            send_g.at[s, :, pl.ds(pl.multiple_of(me * rows, rows), rows), :],
            recv_g.at[s, me],
            own_sem.at[1, s],
        )

    def plane(a):
        half = (ZS - a) // 2
        return (my_z + half * (1 - 2 * ((ZS - 1 - a) % 2)) + ZS) % ZS

    def prepare(s, z):
        def block(array, y):
            return held[s, array, :, pl.ds(pl.multiple_of((z * YS + y) * HD, HD), HD)]

        turned = turn(
            [block(array, y) for array in range(2) for y in range(YS)], tables[s, 0], tables[s, 1]
        )
        scales = planes[s, z]
        for y in range(YS):
            head = z * YS + y
            send_in[s, head, 0] = turned[y]
            send_in[s, head, 1] = turned[YS + y]
            send_in[s, head, 2] = (block(2, y).astype(F32) * scales[:, y : y + 1]).astype(BF16)

    def send(s, z):
        for y in range(YS):
            to = z * YS + y

            @pl.when(to != me)
            def _():
                if s > 0:
                    in_copy(s - 1, to, me).wait_send()
                    t_copy(s, to, me).start()
                in_copy(s, to, me).start()

    def attend(s):
        grad_k[...] = jnp.zeros_like(grad_k)
        grad_v[...] = jnp.zeros_like(grad_v)
        loss_acc[s] = jnp.zeros_like(loss_acc[s])

        @pl.loop(0, LEN // QB)
        def _(b):
            block = pl.ds(pl.multiple_of(b * QB, QB), QB)
            q = recv_in[s, 0, block]
            k = recv_in[s, 1]
            v = recv_in[s, 2]
            scores = lax.dot_general(q, k, (((1,), (1,)), ((), ())), preferred_element_type=F32)
            top = jnp.max(scores, axis=1, keepdims=True)
            e = jnp.exp2((scores - top) * (HD**-0.5 * math.log2(math.e)))
            p = e * (1.0 / jnp.sum(e, axis=1, keepdims=True))
            p_low = p.astype(BF16)
            attended = jnp.dot(p_low, v, preferred_element_type=F32).astype(BF16).astype(F32)
            errors = attended - recv_in[s, 3, block].astype(F32)
            loss_acc[s] += jnp.sum((errors * errors).reshape(QB // 8, 8, HD), axis=0)
            cotangent = errors.astype(BF16)
            delta = jnp.sum(cotangent.astype(F32) * attended, axis=1, keepdims=True)
            grad_v[...] += lax.dot_general(
                p_low, cotangent, (((0,), (0,)), ((), ())), preferred_element_type=F32
            )
            grad_p = lax.dot_general(
                cotangent, v, (((1,), (1,)), ((), ())), preferred_element_type=F32
            )
            grad_s = (p * (grad_p - delta) * HD**-0.5).astype(BF16)
            send_g[s, 0, block] = jnp.dot(grad_s, k, preferred_element_type=F32).astype(BF16)
            grad_k[...] += lax.dot_general(
                grad_s, q, (((0,), (0,)), ((), ())), preferred_element_type=F32
            )

        send_g[s, 1] = grad_k[...].astype(BF16)
        send_g[s, 2] = grad_v[...].astype(BF16)

    def start_g(s, begin, end):
        @pl.loop(begin, end)
        def _(j):
            g_copy(s, n_seq - j).start()

    pl.semaphore_wait(barrier, n_seq + n_dp - 2)

    @pl.loop(1, n_seq)
    def _(j):
        t_copy(0, partner(n_seq - j), me).start()

    for copy in side:
        copy.wait()
    for s in range(samples):
        ready_tables(s)
        t_own(s).start()
    for s in range(samples):
        for array in range(3):
            load(s, array).wait()

        @pl.loop(0, ZS)
        def _(a):
            prepare(s, plane(a))
            send(s, plane(a))

        in_own(s).start()

    @pl.loop(0, samples)
    def _(s):
        wait_in(s)
        attend(s)

        @pl.when(s < last)
        def _():
            @pl.loop(1, n_seq)
            def _(i):
                in_copy(last, (me + i) % n_seq, me).wait_send()

            start_g(s, 1, n_seq)
            g_own(s).start()

    mine = jnp.zeros((8, HD), F32)
    for s in range(samples):
        bucket = bucket_ref[s]
        total = jnp.sum(jnp.sum(loss_acc[s], axis=0, keepdims=True), axis=1, keepdims=True)
        mine += jnp.where(lane == bucket, total / (LEN * width), 0.0)
        mine += jnp.where(lane == bucket + NB, 1.0 / n_seq, 0.0)
    loss_mine[...] = mine

    def dp_copy(i):
        to = (dp + i) % n_dp
        return pltpu.make_async_remote_copy(
            src_ref=loss_mine,
            dst_ref=loss_dp.at[dp],
            send_sem=dp_send.at[i],
            recv_sem=dp_recv.at[dp],
            device_id=(to, me),
            device_id_type=MESH,
        )

    def seq_copy(i):
        to = (me + i) % n_seq
        return pltpu.make_async_remote_copy(
            src_ref=loss_plane,
            dst_ref=loss_seq.at[me],
            send_sem=seq_send.at[i],
            recv_sem=seq_recv.at[me],
            device_id=(dp, to),
            device_id_type=MESH,
        )

    @pl.loop(1, n_dp)
    def _(i):
        dp_copy(i).start()

    loss_dp[dp] = mine
    start_g(last, 1, 2 * n_seq // 3)
    g_own(last).start()

    @pl.loop(1, n_dp)
    def _(i):
        src = (dp + i) % n_dp
        pltpu.make_async_remote_copy(
            src_ref=loss_mine,
            dst_ref=loss_dp.at[src],
            send_sem=dp_send.at[i],
            recv_sem=dp_recv.at[src],
            device_id=(src, me),
            device_id_type=MESH,
        ).wait_recv()

    plane_loss = jnp.sum(loss_dp[...], axis=0)
    loss_plane[...] = plane_loss

    @pl.loop(1, n_seq)
    def _(i):
        seq_copy(i).start()

    loss_seq[me] = plane_loss
    start_g(last, 2 * n_seq // 3, n_seq)

    @pl.loop(1, n_seq)
    def _(i):
        src = (me + i) % n_seq
        pltpu.make_async_remote_copy(
            src_ref=loss_plane,
            dst_ref=loss_seq.at[src],
            send_sem=seq_send.at[i],
            recv_sem=seq_recv.at[src],
            device_id=(dp, src),
            device_id_type=MESH,
        ).wait_recv()

    buckets = jnp.sum(loss_seq[...], axis=0)[0:1, :]
    sum_loss = jnp.sum(jnp.where(lane < NB, buckets, 0.0), axis=1, keepdims=True)
    sum_count = jnp.sum(
        jnp.where((lane >= NB) & (lane < 2 * NB), buckets, 0.0), axis=1, keepdims=True
    )
    mean_all = sum_loss / sum_count

    for s in range(samples):
        bucket = bucket_ref[s]
        chosen_loss = jnp.sum(jnp.where(lane == bucket, buckets, 0.0), axis=1, keepdims=True)
        chosen_count = jnp.sum(
            jnp.where(lane == bucket + NB, buckets, 0.0), axis=1, keepdims=True
        )
        weight = mean_all / (chosen_loss / chosen_count + 1e-5)
        turn_ref[s, 0] = weight * tables[s, 0]
        turn_ref[s, 1] = -weight * tables[s, 1]
        weighed_ref[s] = weight * upright[s]

    results = (
        pltpu.make_async_copy(turn_ref, turn_hbm, side_sem.at[0]),
        pltpu.make_async_copy(weighed_ref, weighed_hbm, side_sem.at[1]),
    )
    for copy in results:
        copy.start()

    for s in range(samples):
        g_own(s).wait()

        @pl.loop(1, n_seq)
        def _(i):
            src = (me + i) % n_seq
            pltpu.make_async_remote_copy(
                src_ref=send_g.at[s, :, pl.ds(pl.multiple_of(src * rows, rows), rows), :],
                dst_ref=recv_g.at[s, src],
                send_sem=g_send.at[s, i],
                recv_sem=g_recv.at[s, src],
                device_id=(dp, src),
                device_id_type=MESH,
            ).wait_recv()

    @pl.loop(1, n_seq)
    def _(i):
        for s in range(samples):
            g_copy(s, i).wait_send()
            t_copy(s, (me + i) % n_seq, me).wait_send()
        seq_copy(i).wait_send()

    @pl.loop(1, n_dp)
    def _(i):
        dp_copy(i).wait_send()

    for copy in results:
        copy.wait()


def finish(
    grad_hbm,
    turn_hbm,
    weighed_hbm,
    oq_hbm,
    ok_hbm,
    ov_hbm,
    grad_ref,
    turn_ref,
    weighed_ref,
    out_ref,
    grad_sem,
    side_sem,
    out_sem,
):
    samples, heads, _, rows, _ = grad_ref.shape
    part = 16
    pieces = 4
    each = heads // pieces

    def load(s, p):
        some = pl.ds(p * each, each)
        return pltpu.make_async_copy(
            grad_hbm.at[s, some], grad_ref.at[s, some], grad_sem.at[s, p]
        )

    side = (
        pltpu.make_async_copy(turn_hbm, turn_ref, side_sem.at[0]),
        pltpu.make_async_copy(weighed_hbm, weighed_ref, side_sem.at[1]),
    )

    def store(s, r, array):
        some = pl.ds(pl.multiple_of(r * part, part), part)
        return pltpu.make_async_copy(
            out_ref.at[array, s, some],
            (oq_hbm, ok_hbm, ov_hbm)[array].at[s, some],
            out_sem.at[array, s, r],
        )

    for p in range(pieces):
        load(0, p).start()
    for copy in side:
        copy.start()
    for s in range(1, samples):
        for p in range(pieces):
            load(s, p).start()
    for copy in side:
        copy.wait()

    @pl.loop(0, samples)
    def _(s):
        for p in range(pieces):
            load(s, p).wait()

        @pl.loop(0, rows // part)
        def _(r):
            some = pl.ds(pl.multiple_of(r * part, part), part)
            for array in range(2):
                turned = turn(
                    [grad_ref[s, h, array, some] for h in range(heads)],
                    turn_ref[s, 0, some],
                    turn_ref[s, 1, some],
                )
                for h in range(heads):
                    out_ref[array, s, some, h * HD : (h + 1) * HD] = turned[h]
                store(s, r, array).start()
            scales = weighed_ref[s, some]
            for h in range(heads):
                out_ref[2, s, some, h * HD : (h + 1) * HD] = (
                    grad_ref[s, h, 2, some].astype(F32) * scales[:, h : h + 1]
                ).astype(BF16)
            store(s, r, 2).start()

    @pl.loop(0, samples)
    def _(s):
        @pl.loop(0, rows // part)
        def _(r):
            for array in range(3):
                store(s, r, array).wait()


def local(n_dp, n_seq, q, k, v, scales, targets, frame_ids, bucket_ids):
    samples, rows, width = q.shape
    exponent = np.arange(HD) % QUARTER / QUARTER
    freq = np.where(np.arange(HD) < 2 * QUARTER, 10000.0 ** (-exponent), 0.0)
    freq = jnp.asarray(freq[None, :], F32)
    scales = jnp.swapaxes(scales, 1, 2)
    smem = pl.BlockSpec(memory_space=pltpu.SMEM)
    anywhere = pl.BlockSpec(memory_space=pl.ANY)
    dma = pltpu.SemaphoreType.DMA
    grads, turns, weighed = pl.pallas_call(
        functools.partial(kernel, n_dp, n_seq),
        out_shape=(
            jax.ShapeDtypeStruct((samples, n_seq, 3, rows, HD), BF16),
            jax.ShapeDtypeStruct((samples, 2, rows, HD), F32),
            jax.ShapeDtypeStruct((samples, rows, n_seq), F32),
        ),
        in_specs=[anywhere] * 7 + [smem],
        out_specs=(anywhere, anywhere, anywhere),
        scratch_shapes=[
            pltpu.VMEM(scales.shape, F32),
            pltpu.VMEM(frame_ids.shape, jnp.int32),
            pltpu.VMEM(freq.shape, F32),
            pltpu.VMEM((samples, 2, rows, HD), F32),
            pltpu.VMEM((samples, rows, n_seq), F32),
            pltpu.VMEM((samples, 3, rows, width), BF16),
            pltpu.VMEM((samples, 2, rows, HD), F32),
            pltpu.VMEM((samples, rows, n_seq), F32),
            pltpu.VMEM((samples, ZS, rows, YS), F32),
            pltpu.VMEM((samples, n_seq, 3, rows, HD), BF16),
            pltpu.VMEM((samples, 4, LEN, HD), BF16),
            pltpu.VMEM((samples, 3, LEN, HD), BF16),
            pltpu.VMEM((LEN, HD), F32),
            pltpu.VMEM((LEN, HD), F32),
            pltpu.VMEM((samples, 8, HD), F32),
            pltpu.VMEM((8, HD), F32),
            pltpu.VMEM((n_dp, 8, HD), F32),
            pltpu.VMEM((8, HD), F32),
            pltpu.VMEM((n_seq, 8, HD), F32),
            dma((samples, n_seq)),
            dma((samples, n_seq)),
            dma((samples, n_seq)),
            dma((samples, n_seq)),
            dma((samples, n_seq)),
            dma((samples, n_seq)),
            dma((n_dp,)),
            dma((n_dp,)),
            dma((n_seq,)),
            dma((n_seq,)),
            dma((3, samples)),
            dma((samples, 3)),
            dma((3,)),
        ],
        compiler_params=pltpu.CompilerParams(
            collective_id=0, has_side_effects=True, vmem_limit_bytes=58 << 20
        ),
    )(q, k, v, targets, scales, frame_ids, freq, bucket_ids)
    out = jax.ShapeDtypeStruct(q.shape, BF16)
    return tuple(
        pl.pallas_call(
            finish,
            out_shape=(out, out, out),
            in_specs=[anywhere] * 3,
            out_specs=(anywhere,) * 3,
            scratch_shapes=[
                pltpu.VMEM(grads.shape, BF16),
                pltpu.VMEM(turns.shape, F32),
                pltpu.VMEM(weighed.shape, F32),
                pltpu.VMEM((3,) + q.shape, BF16),
                dma((samples, 4)),
                dma((2,)),
                dma((3, samples, 4)),
            ],
            compiler_params=pltpu.CompilerParams(vmem_limit_bytes=58 << 20),
        )(grads, turns, weighed)
    )


def solution(mesh):
    spec = P("dp", "seq", None)
    return jax.shard_map(
        functools.partial(local, mesh.shape["dp"], mesh.shape["seq"]),
        mesh=mesh,
        in_specs=(spec, spec, spec, spec, spec, P("dp", "seq"), P("dp")),
        out_specs=(spec, spec, spec),
        check_vma=False,
    )
```

```python
import functools
import math

import jax
import jax.numpy as jnp
import numpy as np
from jax import lax
from jax.experimental import pallas as pl
from jax.experimental.pallas import tpu as pltpu
from jax.sharding import PartitionSpec as P

MESH = pl.DeviceIdType.MESH
HD = 128
LEN = 2048
NB = 8
QUARTER = HD // 4
ZS, YS = 8, 4
QB = 256
GROUP = 8
AHEAD = 8
F32 = jnp.float32
BF16 = jnp.bfloat16


def swap_matrix():
    i = lax.broadcasted_iota(jnp.int32, (HD, HD), 0)
    j = lax.broadcasted_iota(jnp.int32, (HD, HD), 1)
    first = (j < QUARTER) & (i == j + QUARTER)
    second = (j >= QUARTER) & (j < 2 * QUARTER) & (i == j - QUARTER)
    return jnp.where(first | second, 1.0, 0.0).astype(BF16)


def turn(blocks, cosine, sine):
    x = jnp.concatenate(blocks, axis=0)
    swapped = jnp.dot(x, swap_matrix(), preferred_element_type=F32)
    shape = (len(blocks),) + blocks[0].shape
    turned = x.astype(F32).reshape(shape) * cosine + swapped.reshape(shape) * sine
    return turned.astype(BF16)


def kernel(
    n_dp,
    n_seq,
    q_ref,
    k_ref,
    v_ref,
    t_ref,
    scale_hbm,
    frame_hbm,
    freq_hbm,
    bucket_ref,
    recv_g,
    turn_hbm,
    weighed_hbm,
    scale_ref,
    frame_ref,
    freq_ref,
    turn_ref,
    weighed_ref,
    held,
    tables,
    upright,
    planes,
    send_in,
    recv_in,
    send_g,
    grad_k,
    grad_v,
    loss_acc,
    loss_mine,
    loss_dp,
    loss_plane,
    loss_seq,
    in_send,
    in_recv,
    t_send,
    t_recv,
    g_send,
    g_recv,
    dp_send,
    dp_recv,
    seq_send,
    seq_recv,
    own_sem,
    load_sem,
    side_sem,
):
    samples, rows, width = q_ref.shape
    last = samples - 1
    dp = lax.axis_index("dp")
    me = lax.axis_index("seq")
    my_z, my_y = me // YS, me % YS

    def partner(i):
        a, dy = i // YS, i % YS
        half = (a + 1) // 2
        dz = half * (1 - 2 * (a % 2)) + ZS
        return ((my_z + dz) % ZS) * YS + (my_y + dy) % YS

    barrier = pltpu.get_barrier_semaphore()

    @pl.loop(1, n_seq)
    def _(i):
        pl.semaphore_signal(barrier, inc=1, device_id=(dp, (me + i) % n_seq), device_id_type=MESH)

    @pl.loop(1, n_dp)
    def _(i):
        pl.semaphore_signal(barrier, inc=1, device_id=((dp + i) % n_dp, me), device_id_type=MESH)

    side = [
        pltpu.make_async_copy(source, there, side_sem.at[i])
        for i, (source, there) in enumerate(
            ((scale_hbm, scale_ref), (frame_hbm, frame_ref), (freq_hbm, freq_ref))
        )
    ]

    def load(s, array):
        source = (q_ref, k_ref, v_ref)[array]
        return pltpu.make_async_copy(source.at[s], held.at[s, array], load_sem.at[s, array])

    for copy in side:
        copy.start()
    for s in range(samples):
        for array in range(3):
            load(s, array).start()

    lane = lax.broadcasted_iota(jnp.int32, (1, HD), 1)
    eye = lax.broadcasted_iota(jnp.int32, (rows, rows), 0) == lax.broadcasted_iota(
        jnp.int32, (rows, rows), 1
    )

    def ready_tables(s):
        ids = frame_ref[s : s + 1, :].astype(F32)
        angle = jnp.sum(jnp.where(eye, ids, 0.0), axis=1, keepdims=True) * freq_ref[...]
        tables[s, 0] = jnp.where(lane < 2 * QUARTER, jnp.cos(angle), 1.0)
        sine = jnp.sin(angle)
        tables[s, 1] = jnp.where(
            lane < QUARTER, -sine, jnp.where(lane < 2 * QUARTER, sine, 0.0)
        )
        columns = jnp.transpose(scale_ref[s])
        upright[s] = columns
        for z in range(ZS):
            planes[s, z] = columns[:, z * YS : (z + 1) * YS]

    def rows_of(device):
        return pl.ds(pl.multiple_of(device * rows, rows), rows)

    def head_of(device):
        return pl.ds(pl.multiple_of(device * HD, HD), HD)

    def in_copy(s, to, source):
        return pltpu.make_async_remote_copy(
            src_ref=send_in.at[s, to],
            dst_ref=recv_in.at[s, pl.ds(0, 3), rows_of(source), :],
            send_sem=in_send.at[s, to],
            recv_sem=in_recv.at[s, source],
            device_id=(dp, to),
            device_id_type=MESH,
        )

    def t_copy(s, to, source):
        return pltpu.make_async_remote_copy(
            src_ref=t_ref.at[s, :, head_of(to)],
            dst_ref=recv_in.at[s, 3, rows_of(source), :],
            send_sem=t_send.at[s, to],
            recv_sem=t_recv.at[s, source],
            device_id=(dp, to),
            device_id_type=MESH,
        )

    def in_own(s):
        return pltpu.make_async_copy(
            send_in.at[s, me], recv_in.at[s, pl.ds(0, 3), rows_of(me), :], own_sem.at[0, s]
        )

    def t_own(s):
        return pltpu.make_async_copy(
            t_ref.at[s, :, head_of(me)], recv_in.at[s, 3, rows_of(me), :], own_sem.at[2, s]
        )

    def wait_in(s):
        @pl.loop(1, n_seq)
        def _(i):
            source = (me + i) % n_seq
            t_copy(s, source, source).wait_recv()
            in_copy(s, source, source).wait_recv()

        in_own(s).wait()
        t_own(s).wait()

    def g_copy(s, i):
        to = partner(i)
        return pltpu.make_async_remote_copy(
            src_ref=send_g.at[s, :, pl.ds(pl.multiple_of(to * rows, rows), rows), :],
            dst_ref=recv_g.at[s, me],
            send_sem=g_send.at[s, i],
            recv_sem=g_recv.at[s, me],
            device_id=(dp, to),
            device_id_type=MESH,
        )

    def g_own(s):
        return pltpu.make_async_copy(
            send_g.at[s, :, pl.ds(pl.multiple_of(me * rows, rows), rows), :],
            recv_g.at[s, me],
            own_sem.at[1, s],
        )

    def plane(a):
        half = (ZS - a) // 2
        return (my_z + half * (1 - 2 * ((ZS - 1 - a) % 2)) + ZS) % ZS

    def prepare(s, z):
        def block(array, y):
            return held[s, array, :, pl.ds(pl.multiple_of((z * YS + y) * HD, HD), HD)]

        turned = turn(
            [block(array, y) for array in range(2) for y in range(YS)], tables[s, 0], tables[s, 1]
        )
        scales = planes[s, z]
        for y in range(YS):
            head = z * YS + y
            send_in[s, head, 0] = turned[y]
            send_in[s, head, 1] = turned[YS + y]
            send_in[s, head, 2] = (block(2, y).astype(F32) * scales[:, y : y + 1]).astype(BF16)

    def send(s, z):
        for y in range(YS):
            to = z * YS + y

            @pl.when(to != me)
            def _():
                if s > 0:
                    in_copy(s - 1, to, me).wait_send()
                    t_copy(s, to, me).start()
                in_copy(s, to, me).start()

    def attend(s):
        grad_k[...] = jnp.zeros_like(grad_k)
        grad_v[...] = jnp.zeros_like(grad_v)
        loss_acc[s] = jnp.zeros_like(loss_acc[s])

        @pl.loop(0, LEN // QB)
        def _(b):
            block = pl.ds(pl.multiple_of(b * QB, QB), QB)
            q = recv_in[s, 0, block]
            k = recv_in[s, 1]
            v = recv_in[s, 2]
            scores = lax.dot_general(q, k, (((1,), (1,)), ((), ())), preferred_element_type=F32)
            top = jnp.max(scores, axis=1, keepdims=True)
            e = jnp.exp2((scores - top) * (HD**-0.5 * math.log2(math.e)))
            p = e * (1.0 / jnp.sum(e, axis=1, keepdims=True))
            p_low = p.astype(BF16)
            attended = jnp.dot(p_low, v, preferred_element_type=F32).astype(BF16).astype(F32)
            errors = attended - recv_in[s, 3, block].astype(F32)
            loss_acc[s] += jnp.sum((errors * errors).reshape(QB // 8, 8, HD), axis=0)
            cotangent = errors.astype(BF16)
            delta = jnp.sum(cotangent.astype(F32) * attended, axis=1, keepdims=True)
            grad_v[...] += lax.dot_general(
                p_low, cotangent, (((0,), (0,)), ((), ())), preferred_element_type=F32
            )
            grad_p = lax.dot_general(
                cotangent, v, (((1,), (1,)), ((), ())), preferred_element_type=F32
            )
            grad_s = (p * (grad_p - delta) * HD**-0.5).astype(BF16)
            send_g[s, 0, block] = jnp.dot(grad_s, k, preferred_element_type=F32).astype(BF16)
            grad_k[...] += lax.dot_general(
                grad_s, q, (((0,), (0,)), ((), ())), preferred_element_type=F32
            )

        send_g[s, 1] = grad_k[...].astype(BF16)
        send_g[s, 2] = grad_v[...].astype(BF16)

    def start_g(s, begin, end):
        @pl.loop(begin, end)
        def _(j):
            g_copy(s, n_seq - j).start()

    pl.semaphore_wait(barrier, n_seq + n_dp - 2)

    @pl.loop(1, n_seq)
    def _(j):
        t_copy(0, partner(n_seq - j), me).start()

    for copy in side:
        copy.wait()
    for s in range(samples):
        ready_tables(s)
        t_own(s).start()
    for s in range(samples):
        for array in range(3):
            load(s, array).wait()

        @pl.loop(0, ZS)
        def _(a):
            prepare(s, plane(a))
            send(s, plane(a))

        in_own(s).start()

    @pl.loop(0, samples)
    def _(s):
        wait_in(s)
        attend(s)

        @pl.when(s < last)
        def _():
            start_g(s, 1, AHEAD + 1)

            @pl.loop(1, n_seq - AHEAD)
            def _(j):
                in_copy(last, partner(n_seq - j), me).wait_send()
                g_copy(s, n_seq - AHEAD - j).start()

            @pl.loop(n_seq - AHEAD, n_seq)
            def _(j):
                in_copy(last, partner(n_seq - j), me).wait_send()

            g_own(s).start()

    mine = jnp.zeros((1, HD), F32)
    for s in range(samples):
        bucket = bucket_ref[s]
        total = jnp.sum(jnp.sum(loss_acc[s], axis=0, keepdims=True), axis=1, keepdims=True)
        mine += jnp.where(lane == bucket, total / (LEN * width), 0.0)
        mine += jnp.where(lane == bucket + NB, 1.0 / n_seq, 0.0)
    loss_mine[...] = mine

    def dp_copy(i):
        to = (dp + i) % n_dp
        return pltpu.make_async_remote_copy(
            src_ref=loss_mine,
            dst_ref=loss_dp.at[dp],
            send_sem=dp_send.at[i],
            recv_sem=dp_recv.at[dp],
            device_id=(to, me),
            device_id_type=MESH,
        )

    def seq_copy(i):
        to = (me + i) % n_seq
        return pltpu.make_async_remote_copy(
            src_ref=loss_plane,
            dst_ref=loss_seq.at[me],
            send_sem=seq_send.at[i],
            recv_sem=seq_recv.at[me],
            device_id=(dp, to),
            device_id_type=MESH,
        )

    @pl.loop(1, n_dp)
    def _(i):
        dp_copy(i).start()

    loss_dp[dp] = mine
    start_g(last, 1, 2 * n_seq // 3)
    g_own(last).start()

    @pl.loop(1, n_dp)
    def _(i):
        src = (dp + i) % n_dp
        pltpu.make_async_remote_copy(
            src_ref=loss_mine,
            dst_ref=loss_dp.at[src],
            send_sem=dp_send.at[i],
            recv_sem=dp_recv.at[src],
            device_id=(src, me),
            device_id_type=MESH,
        ).wait_recv()

    plane_loss = jnp.sum(loss_dp[...], axis=0)
    loss_plane[...] = plane_loss

    @pl.loop(1, n_seq)
    def _(i):
        seq_copy(i).start()

    loss_seq[me] = plane_loss
    start_g(last, 2 * n_seq // 3, n_seq)

    @pl.loop(1, n_seq)
    def _(i):
        src = (me + i) % n_seq
        pltpu.make_async_remote_copy(
            src_ref=loss_plane,
            dst_ref=loss_seq.at[src],
            send_sem=seq_send.at[i],
            recv_sem=seq_recv.at[src],
            device_id=(dp, src),
            device_id_type=MESH,
        ).wait_recv()

    buckets = jnp.sum(loss_seq[...], axis=0)
    sum_loss = jnp.sum(jnp.where(lane < NB, buckets, 0.0), axis=1, keepdims=True)
    sum_count = jnp.sum(
        jnp.where((lane >= NB) & (lane < 2 * NB), buckets, 0.0), axis=1, keepdims=True
    )
    mean_all = sum_loss / sum_count

    for s in range(samples):
        bucket = bucket_ref[s]
        chosen_loss = jnp.sum(jnp.where(lane == bucket, buckets, 0.0), axis=1, keepdims=True)
        chosen_count = jnp.sum(
            jnp.where(lane == bucket + NB, buckets, 0.0), axis=1, keepdims=True
        )
        weight = mean_all / (chosen_loss / chosen_count + 1e-5)
        turn_ref[s, 0] = weight * tables[s, 0]
        turn_ref[s, 1] = -weight * tables[s, 1]
        weighed = weight * upright[s]
        for g in range(n_seq // GROUP):
            weighed_ref[s, g] = weighed[:, g * GROUP : (g + 1) * GROUP]

    results = (
        pltpu.make_async_copy(turn_ref, turn_hbm, side_sem.at[0]),
        pltpu.make_async_copy(weighed_ref, weighed_hbm, side_sem.at[1]),
    )
    for copy in results:
        copy.start()

    for s in range(samples):
        g_own(s).wait()

        @pl.loop(1, n_seq)
        def _(i):
            src = (me + i) % n_seq
            pltpu.make_async_remote_copy(
                src_ref=send_g.at[s, :, pl.ds(pl.multiple_of(src * rows, rows), rows), :],
                dst_ref=recv_g.at[s, src],
                send_sem=g_send.at[s, i],
                recv_sem=g_recv.at[s, src],
                device_id=(dp, src),
                device_id_type=MESH,
            ).wait_recv()

    @pl.loop(1, n_seq)
    def _(i):
        for s in range(samples):
            g_copy(s, i).wait_send()
            t_copy(s, (me + i) % n_seq, me).wait_send()
        seq_copy(i).wait_send()

    @pl.loop(1, n_dp)
    def _(i):
        dp_copy(i).wait_send()

    for copy in results:
        copy.wait()


def finish(
    grad_hbm,
    turn_hbm,
    weighed_hbm,
    oq_hbm,
    ok_hbm,
    ov_hbm,
    grad_ref,
    turn_ref,
    weighed_ref,
    out_ref,
    grad_sem,
    side_sem,
    out_sem,
):
    samples, heads = grad_ref.shape[:2]
    groups = heads // GROUP

    def load(s, g):
        some = pl.ds(g * GROUP, GROUP)
        return pltpu.make_async_copy(
            grad_hbm.at[s, some], grad_ref.at[s, some], grad_sem.at[s, g]
        )

    def store(s, g, array):
        some = pl.ds(pl.multiple_of(g * (GROUP * HD), GROUP * HD), GROUP * HD)
        return pltpu.make_async_copy(
            out_ref.at[array, s, :, some],
            (oq_hbm, ok_hbm, ov_hbm)[array].at[s, :, some],
            out_sem.at[array, s, g],
        )

    side = (
        pltpu.make_async_copy(turn_hbm, turn_ref, side_sem.at[0]),
        pltpu.make_async_copy(weighed_hbm, weighed_ref, side_sem.at[1]),
    )
    for copy in side:
        copy.start()

    @pl.loop(0, samples * groups)
    def _(i):
        load(i // groups, i % groups).start()

    for copy in side:
        copy.wait()

    @pl.loop(0, samples * groups)
    def _(i):
        s, g = i // groups, i % groups
        load(s, g).wait()

        def columns(h):
            return pl.ds(pl.multiple_of((g * GROUP + h) * HD, HD), HD)

        for array in range(2):
            turned = turn(
                [grad_ref[s, g * GROUP + h, array] for h in range(GROUP)],
                turn_ref[s, 0],
                turn_ref[s, 1],
            )
            for h in range(GROUP):
                out_ref[array, s, :, columns(h)] = turned[h]
            store(s, g, array).start()
        scales = weighed_ref[s, g]
        for h in range(GROUP):
            out_ref[2, s, :, columns(h)] = (
                grad_ref[s, g * GROUP + h, 2].astype(F32) * scales[:, h : h + 1]
            ).astype(BF16)
        store(s, g, 2).start()

    @pl.loop(0, samples * groups)
    def _(i):
        for array in range(3):
            store(i // groups, i % groups, array).wait()


def local(n_dp, n_seq, q, k, v, scales, targets, frame_ids, bucket_ids):
    samples, rows, width = q.shape
    exponent = np.arange(HD) % QUARTER / QUARTER
    freq = np.where(np.arange(HD) < 2 * QUARTER, 10000.0 ** (-exponent), 0.0)
    freq = jnp.asarray(freq[None, :], F32)
    scales = jnp.swapaxes(scales, 1, 2)
    smem = pl.BlockSpec(memory_space=pltpu.SMEM)
    anywhere = pl.BlockSpec(memory_space=pl.ANY)
    dma = pltpu.SemaphoreType.DMA
    grads, turns, weighed = pl.pallas_call(
        functools.partial(kernel, n_dp, n_seq),
        out_shape=(
            jax.ShapeDtypeStruct((samples, n_seq, 3, rows, HD), BF16),
            jax.ShapeDtypeStruct((samples, 2, rows, HD), F32),
            jax.ShapeDtypeStruct((samples, n_seq // GROUP, rows, GROUP), F32),
        ),
        in_specs=[anywhere] * 7 + [smem],
        out_specs=(anywhere, anywhere, anywhere),
        scratch_shapes=[
            pltpu.VMEM(scales.shape, F32),
            pltpu.VMEM(frame_ids.shape, jnp.int32),
            pltpu.VMEM(freq.shape, F32),
            pltpu.VMEM((samples, 2, rows, HD), F32),
            pltpu.VMEM((samples, n_seq // GROUP, rows, GROUP), F32),
            pltpu.VMEM((samples, 3, rows, width), BF16),
            pltpu.VMEM((samples, 2, rows, HD), F32),
            pltpu.VMEM((samples, rows, n_seq), F32),
            pltpu.VMEM((samples, ZS, rows, YS), F32),
            pltpu.VMEM((samples, n_seq, 3, rows, HD), BF16),
            pltpu.VMEM((samples, 4, LEN, HD), BF16),
            pltpu.VMEM((samples, 3, LEN, HD), BF16),
            pltpu.VMEM((LEN, HD), F32),
            pltpu.VMEM((LEN, HD), F32),
            pltpu.VMEM((samples, 8, HD), F32),
            pltpu.VMEM((1, HD), F32),
            pltpu.VMEM((n_dp, 1, HD), F32),
            pltpu.VMEM((1, HD), F32),
            pltpu.VMEM((n_seq, 1, HD), F32),
            dma((samples, n_seq)),
            dma((samples, n_seq)),
            dma((samples, n_seq)),
            dma((samples, n_seq)),
            dma((samples, n_seq)),
            dma((samples, n_seq)),
            dma((n_dp,)),
            dma((n_dp,)),
            dma((n_seq,)),
            dma((n_seq,)),
            dma((3, samples)),
            dma((samples, 3)),
            dma((3,)),
        ],
        compiler_params=pltpu.CompilerParams(
            collective_id=0, has_side_effects=True, vmem_limit_bytes=58 << 20
        ),
    )(q, k, v, targets, scales, frame_ids, freq, bucket_ids)
    out = jax.ShapeDtypeStruct(q.shape, BF16)
    return tuple(
        pl.pallas_call(
            finish,
            out_shape=(out, out, out),
            in_specs=[anywhere] * 3,
            out_specs=(anywhere,) * 3,
            scratch_shapes=[
                pltpu.VMEM(grads.shape, BF16),
                pltpu.VMEM(turns.shape, F32),
                pltpu.VMEM(weighed.shape, F32),
                pltpu.VMEM((3,) + q.shape, BF16),
                dma((samples, n_seq // GROUP)),
                dma((2,)),
                dma((3, samples, n_seq // GROUP)),
            ],
            compiler_params=pltpu.CompilerParams(vmem_limit_bytes=58 << 20),
        )(grads, turns, weighed)
    )


def solution(mesh):
    spec = P("dp", "seq", None)
    return jax.shard_map(
        functools.partial(local, mesh.shape["dp"], mesh.shape["seq"]),
        mesh=mesh,
        in_specs=(spec, spec, spec, spec, spec, P("dp", "seq"), P("dp")),
        out_specs=(spec, spec, spec),
        check_vma=False,
    )
```

```python
import functools
import math

import jax
import jax.numpy as jnp
import numpy as np
from jax import lax
from jax.experimental import pallas as pl
from jax.experimental.pallas import tpu as pltpu
from jax.sharding import PartitionSpec as P

MESH = pl.DeviceIdType.MESH
HD = 128
LEN = 2048
NB = 8
QUARTER = HD // 4
ZS, YS = 8, 4
QB = 256
GROUP = 8
AHEAD = 8
F32 = jnp.float32
BF16 = jnp.bfloat16


def swap_matrix():
    i = lax.broadcasted_iota(jnp.int32, (HD, HD), 0)
    j = lax.broadcasted_iota(jnp.int32, (HD, HD), 1)
    first = (j < QUARTER) & (i == j + QUARTER)
    second = (j >= QUARTER) & (j < 2 * QUARTER) & (i == j - QUARTER)
    return jnp.where(first | second, 1.0, 0.0).astype(BF16)


def turn(blocks, cosine, sine):
    x = jnp.concatenate(blocks, axis=0)
    swapped = jnp.dot(x, swap_matrix(), preferred_element_type=F32)
    shape = (len(blocks),) + blocks[0].shape
    turned = x.astype(F32).reshape(shape) * cosine + swapped.reshape(shape) * sine
    return turned.astype(BF16)


def kernel(
    n_dp,
    n_seq,
    q_ref,
    k_ref,
    v_ref,
    t_ref,
    scale_hbm,
    frame_hbm,
    freq_hbm,
    bucket_ref,
    recv_g,
    turn_hbm,
    weighed_hbm,
    scale_ref,
    frame_ref,
    freq_ref,
    turn_ref,
    weighed_ref,
    held,
    tables,
    upright,
    planes,
    send_in,
    recv_in,
    send_g,
    grad_k,
    grad_v,
    loss_acc,
    loss_mine,
    loss_dp,
    loss_plane,
    loss_seq,
    in_send,
    in_recv,
    t_send,
    t_recv,
    g_send,
    g_recv,
    dp_send,
    dp_recv,
    seq_send,
    seq_recv,
    own_sem,
    load_sem,
    side_sem,
):
    samples, rows, width = q_ref.shape
    last = samples - 1
    dp = lax.axis_index("dp")
    me = lax.axis_index("seq")
    my_z, my_y = me // YS, me % YS

    def partner(i):
        a, dy = i % ZS, i // ZS
        half = (a + 1) // 2
        dz = half * (1 - 2 * (a % 2)) + ZS
        return ((my_z + dz) % ZS) * YS + (my_y + dy + half) % YS

    barrier = pltpu.get_barrier_semaphore()

    @pl.loop(1, n_seq)
    def _(i):
        pl.semaphore_signal(barrier, inc=1, device_id=(dp, (me + i) % n_seq), device_id_type=MESH)

    @pl.loop(1, n_dp)
    def _(i):
        pl.semaphore_signal(barrier, inc=1, device_id=((dp + i) % n_dp, me), device_id_type=MESH)

    side = [
        pltpu.make_async_copy(source, there, side_sem.at[i])
        for i, (source, there) in enumerate(
            ((scale_hbm, scale_ref), (frame_hbm, frame_ref), (freq_hbm, freq_ref))
        )
    ]

    def load(s, array):
        source = (q_ref, k_ref, v_ref)[array]
        return pltpu.make_async_copy(source.at[s], held.at[s, array], load_sem.at[s, array])

    for copy in side:
        copy.start()
    for s in range(samples):
        for array in range(3):
            load(s, array).start()

    lane = lax.broadcasted_iota(jnp.int32, (1, HD), 1)
    eye = lax.broadcasted_iota(jnp.int32, (rows, rows), 0) == lax.broadcasted_iota(
        jnp.int32, (rows, rows), 1
    )

    def ready_tables(s):
        ids = frame_ref[s : s + 1, :].astype(F32)
        angle = jnp.sum(jnp.where(eye, ids, 0.0), axis=1, keepdims=True) * freq_ref[...]
        tables[s, 0] = jnp.where(lane < 2 * QUARTER, jnp.cos(angle), 1.0)
        sine = jnp.sin(angle)
        tables[s, 1] = jnp.where(
            lane < QUARTER, -sine, jnp.where(lane < 2 * QUARTER, sine, 0.0)
        )
        columns = jnp.transpose(scale_ref[s])
        upright[s] = columns
        for z in range(ZS):
            planes[s, z] = columns[:, z * YS : (z + 1) * YS]

    def rows_of(device):
        return pl.ds(pl.multiple_of(device * rows, rows), rows)

    def head_of(device):
        return pl.ds(pl.multiple_of(device * HD, HD), HD)

    def in_copy(s, to, source):
        return pltpu.make_async_remote_copy(
            src_ref=send_in.at[s, to],
            dst_ref=recv_in.at[s, pl.ds(0, 3), rows_of(source), :],
            send_sem=in_send.at[s, to],
            recv_sem=in_recv.at[s, source],
            device_id=(dp, to),
            device_id_type=MESH,
        )

    def t_copy(s, to, source):
        return pltpu.make_async_remote_copy(
            src_ref=t_ref.at[s, :, head_of(to)],
            dst_ref=recv_in.at[s, 3, rows_of(source), :],
            send_sem=t_send.at[s, to],
            recv_sem=t_recv.at[s, source],
            device_id=(dp, to),
            device_id_type=MESH,
        )

    def in_own(s):
        return pltpu.make_async_copy(
            send_in.at[s, me], recv_in.at[s, pl.ds(0, 3), rows_of(me), :], own_sem.at[0, s]
        )

    def t_own(s):
        return pltpu.make_async_copy(
            t_ref.at[s, :, head_of(me)], recv_in.at[s, 3, rows_of(me), :], own_sem.at[2, s]
        )

    def wait_in(s):
        @pl.loop(1, n_seq)
        def _(i):
            source = (me + i) % n_seq
            t_copy(s, source, source).wait_recv()
            in_copy(s, source, source).wait_recv()

        in_own(s).wait()
        t_own(s).wait()

    def g_copy(s, i):
        to = partner(i)
        return pltpu.make_async_remote_copy(
            src_ref=send_g.at[s, :, pl.ds(pl.multiple_of(to * rows, rows), rows), :],
            dst_ref=recv_g.at[s, me],
            send_sem=g_send.at[s, i],
            recv_sem=g_recv.at[s, me],
            device_id=(dp, to),
            device_id_type=MESH,
        )

    def g_own(s):
        return pltpu.make_async_copy(
            send_g.at[s, :, pl.ds(pl.multiple_of(me * rows, rows), rows), :],
            recv_g.at[s, me],
            own_sem.at[1, s],
        )

    def prepare(s, z):
        def block(array, y):
            return held[s, array, :, pl.ds(pl.multiple_of((z * YS + y) * HD, HD), HD)]

        turned = turn(
            [block(array, y) for array in range(2) for y in range(YS)], tables[s, 0], tables[s, 1]
        )
        scales = planes[s, z]
        for y in range(YS):
            head = z * YS + y
            send_in[s, head, 0] = turned[y]
            send_in[s, head, 1] = turned[YS + y]
            send_in[s, head, 2] = (block(2, y).astype(F32) * scales[:, y : y + 1]).astype(BF16)

    def attend(s):
        grad_k[...] = jnp.zeros_like(grad_k)
        grad_v[...] = jnp.zeros_like(grad_v)
        loss_acc[s] = jnp.zeros_like(loss_acc[s])

        @pl.loop(0, LEN // QB)
        def _(b):
            block = pl.ds(pl.multiple_of(b * QB, QB), QB)
            q = recv_in[s, 0, block]
            k = recv_in[s, 1]
            v = recv_in[s, 2]
            scores = lax.dot_general(q, k, (((1,), (1,)), ((), ())), preferred_element_type=F32)
            top = jnp.max(scores, axis=1, keepdims=True)
            e = jnp.exp2((scores - top) * (HD**-0.5 * math.log2(math.e)))
            p = e * (1.0 / jnp.sum(e, axis=1, keepdims=True))
            p_low = p.astype(BF16)
            attended = jnp.dot(p_low, v, preferred_element_type=F32).astype(BF16).astype(F32)
            errors = attended - recv_in[s, 3, block].astype(F32)
            loss_acc[s] += jnp.sum((errors * errors).reshape(QB // 8, 8, HD), axis=0)
            cotangent = errors.astype(BF16)
            delta = jnp.sum(cotangent.astype(F32) * attended, axis=1, keepdims=True)
            grad_v[...] += lax.dot_general(
                p_low, cotangent, (((0,), (0,)), ((), ())), preferred_element_type=F32
            )
            grad_p = lax.dot_general(
                cotangent, v, (((1,), (1,)), ((), ())), preferred_element_type=F32
            )
            grad_s = (p * (grad_p - delta) * HD**-0.5).astype(BF16)
            send_g[s, 0, block] = jnp.dot(grad_s, k, preferred_element_type=F32).astype(BF16)
            grad_k[...] += lax.dot_general(
                grad_s, q, (((0,), (0,)), ((), ())), preferred_element_type=F32
            )

        send_g[s, 1] = grad_k[...].astype(BF16)
        send_g[s, 2] = grad_v[...].astype(BF16)

    def start_g(s, begin, end):
        @pl.loop(begin, end)
        def _(j):
            g_copy(s, n_seq - j).start()

    pl.semaphore_wait(barrier, n_seq + n_dp - 2)

    @pl.loop(1, n_seq)
    def _(j):
        t_copy(0, partner(n_seq - j), me).start()

    for copy in side:
        copy.wait()
    for s in range(samples):
        ready_tables(s)
        t_own(s).start()
        for array in range(3):
            load(s, array).wait()

        @pl.loop(0, ZS)
        def _(z):
            prepare(s, z)

        if s == 0:

            @pl.loop(1, n_seq)
            def _(j):
                in_copy(s, partner(n_seq - j), me).start()

        else:

            @pl.loop(1, n_seq)
            def _(j):
                to = partner(n_seq - j)
                in_copy(s - 1, to, me).wait_send()
                t_copy(s, to, me).start()
                in_copy(s, to, me).start()

        in_own(s).start()

    @pl.loop(0, samples)
    def _(s):
        wait_in(s)
        attend(s)

        @pl.when(s < last)
        def _():
            start_g(s, 1, AHEAD + 1)

            @pl.loop(1, n_seq - AHEAD)
            def _(j):
                in_copy(last, partner(n_seq - j), me).wait_send()
                g_copy(s, n_seq - AHEAD - j).start()

            @pl.loop(n_seq - AHEAD, n_seq)
            def _(j):
                in_copy(last, partner(n_seq - j), me).wait_send()

            g_own(s).start()

    mine = jnp.zeros((1, HD), F32)
    for s in range(samples):
        bucket = bucket_ref[s]
        total = jnp.sum(jnp.sum(loss_acc[s], axis=0, keepdims=True), axis=1, keepdims=True)
        mine += jnp.where(lane == bucket, total / (LEN * width), 0.0)
        mine += jnp.where(lane == bucket + NB, 1.0 / n_seq, 0.0)
    loss_mine[...] = mine

    def dp_copy(i):
        to = (dp + i) % n_dp
        return pltpu.make_async_remote_copy(
            src_ref=loss_mine,
            dst_ref=loss_dp.at[dp],
            send_sem=dp_send.at[i],
            recv_sem=dp_recv.at[dp],
            device_id=(to, me),
            device_id_type=MESH,
        )

    def seq_copy(i):
        to = (me + i) % n_seq
        return pltpu.make_async_remote_copy(
            src_ref=loss_plane,
            dst_ref=loss_seq.at[me],
            send_sem=seq_send.at[i],
            recv_sem=seq_recv.at[me],
            device_id=(dp, to),
            device_id_type=MESH,
        )

    @pl.loop(1, n_dp)
    def _(i):
        dp_copy(i).start()

    loss_dp[dp] = mine
    start_g(last, 1, 2 * n_seq // 3)
    g_own(last).start()

    @pl.loop(1, n_dp)
    def _(i):
        src = (dp + i) % n_dp
        pltpu.make_async_remote_copy(
            src_ref=loss_mine,
            dst_ref=loss_dp.at[src],
            send_sem=dp_send.at[i],
            recv_sem=dp_recv.at[src],
            device_id=(src, me),
            device_id_type=MESH,
        ).wait_recv()

    plane_loss = jnp.sum(loss_dp[...], axis=0)
    loss_plane[...] = plane_loss

    @pl.loop(1, n_seq)
    def _(i):
        seq_copy(i).start()

    loss_seq[me] = plane_loss
    start_g(last, 2 * n_seq // 3, n_seq)

    @pl.loop(1, n_seq)
    def _(i):
        src = (me + i) % n_seq
        pltpu.make_async_remote_copy(
            src_ref=loss_plane,
            dst_ref=loss_seq.at[src],
            send_sem=seq_send.at[i],
            recv_sem=seq_recv.at[src],
            device_id=(dp, src),
            device_id_type=MESH,
        ).wait_recv()

    buckets = jnp.sum(loss_seq[...], axis=0)
    sum_loss = jnp.sum(jnp.where(lane < NB, buckets, 0.0), axis=1, keepdims=True)
    sum_count = jnp.sum(
        jnp.where((lane >= NB) & (lane < 2 * NB), buckets, 0.0), axis=1, keepdims=True
    )
    mean_all = sum_loss / sum_count

    for s in range(samples):
        bucket = bucket_ref[s]
        chosen_loss = jnp.sum(jnp.where(lane == bucket, buckets, 0.0), axis=1, keepdims=True)
        chosen_count = jnp.sum(
            jnp.where(lane == bucket + NB, buckets, 0.0), axis=1, keepdims=True
        )
        weight = mean_all / (chosen_loss / chosen_count + 1e-5)
        turn_ref[s, 0] = weight * tables[s, 0]
        turn_ref[s, 1] = -weight * tables[s, 1]
        weighed = weight * upright[s]
        for g in range(n_seq // GROUP):
            weighed_ref[s, g] = weighed[:, g * GROUP : (g + 1) * GROUP]

    results = (
        pltpu.make_async_copy(turn_ref, turn_hbm, side_sem.at[0]),
        pltpu.make_async_copy(weighed_ref, weighed_hbm, side_sem.at[1]),
    )
    for copy in results:
        copy.start()

    for s in range(samples):
        g_own(s).wait()

        @pl.loop(1, n_seq)
        def _(i):
            src = (me + i) % n_seq
            pltpu.make_async_remote_copy(
                src_ref=send_g.at[s, :, pl.ds(pl.multiple_of(src * rows, rows), rows), :],
                dst_ref=recv_g.at[s, src],
                send_sem=g_send.at[s, i],
                recv_sem=g_recv.at[s, src],
                device_id=(dp, src),
                device_id_type=MESH,
            ).wait_recv()

    @pl.loop(1, n_seq)
    def _(i):
        for s in range(samples):
            g_copy(s, i).wait_send()
            t_copy(s, (me + i) % n_seq, me).wait_send()
        seq_copy(i).wait_send()

    @pl.loop(1, n_dp)
    def _(i):
        dp_copy(i).wait_send()

    for copy in results:
        copy.wait()


def finish(
    grad_hbm,
    turn_hbm,
    weighed_hbm,
    oq_hbm,
    ok_hbm,
    ov_hbm,
    grad_ref,
    turn_ref,
    weighed_ref,
    out_ref,
    grad_sem,
    side_sem,
    out_sem,
):
    samples, heads = grad_ref.shape[:2]
    groups = heads // GROUP

    def load(s, g):
        some = pl.ds(g * GROUP, GROUP)
        return pltpu.make_async_copy(
            grad_hbm.at[s, some], grad_ref.at[s, some], grad_sem.at[s, g]
        )

    def store(s, g, array):
        some = pl.ds(pl.multiple_of(g * (GROUP * HD), GROUP * HD), GROUP * HD)
        return pltpu.make_async_copy(
            out_ref.at[array, s, :, some],
            (oq_hbm, ok_hbm, ov_hbm)[array].at[s, :, some],
            out_sem.at[array, s, g],
        )

    side = (
        pltpu.make_async_copy(turn_hbm, turn_ref, side_sem.at[0]),
        pltpu.make_async_copy(weighed_hbm, weighed_ref, side_sem.at[1]),
    )
    for copy in side:
        copy.start()

    @pl.loop(0, samples * groups)
    def _(i):
        load(i // groups, i % groups).start()

    for copy in side:
        copy.wait()

    @pl.loop(0, samples * groups)
    def _(i):
        s, g = i // groups, i % groups
        load(s, g).wait()

        def columns(h):
            return pl.ds(pl.multiple_of((g * GROUP + h) * HD, HD), HD)

        turned = turn(
            [grad_ref[s, g * GROUP + h, array] for array in range(2) for h in range(GROUP)],
            turn_ref[s, 0],
            turn_ref[s, 1],
        )
        for array in range(2):
            for h in range(GROUP):
                out_ref[array, s, :, columns(h)] = turned[array * GROUP + h]
            store(s, g, array).start()
        scales = weighed_ref[s, g]
        for h in range(GROUP):
            out_ref[2, s, :, columns(h)] = (
                grad_ref[s, g * GROUP + h, 2].astype(F32) * scales[:, h : h + 1]
            ).astype(BF16)
        store(s, g, 2).start()

    @pl.loop(0, samples * groups)
    def _(i):
        for array in range(3):
            store(i // groups, i % groups, array).wait()


def local(n_dp, n_seq, q, k, v, scales, targets, frame_ids, bucket_ids):
    samples, rows, width = q.shape
    exponent = np.arange(HD) % QUARTER / QUARTER
    freq = np.where(np.arange(HD) < 2 * QUARTER, 10000.0 ** (-exponent), 0.0)
    freq = jnp.asarray(freq[None, :], F32)
    scales = jnp.swapaxes(scales, 1, 2)
    smem = pl.BlockSpec(memory_space=pltpu.SMEM)
    anywhere = pl.BlockSpec(memory_space=pl.ANY)
    dma = pltpu.SemaphoreType.DMA
    grads, turns, weighed = pl.pallas_call(
        functools.partial(kernel, n_dp, n_seq),
        out_shape=(
            jax.ShapeDtypeStruct((samples, n_seq, 3, rows, HD), BF16),
            jax.ShapeDtypeStruct((samples, 2, rows, HD), F32),
            jax.ShapeDtypeStruct((samples, n_seq // GROUP, rows, GROUP), F32),
        ),
        in_specs=[anywhere] * 7 + [smem],
        out_specs=(anywhere, anywhere, anywhere),
        scratch_shapes=[
            pltpu.VMEM(scales.shape, F32),
            pltpu.VMEM(frame_ids.shape, jnp.int32),
            pltpu.VMEM(freq.shape, F32),
            pltpu.VMEM((samples, 2, rows, HD), F32),
            pltpu.VMEM((samples, n_seq // GROUP, rows, GROUP), F32),
            pltpu.VMEM((samples, 3, rows, width), BF16),
            pltpu.VMEM((samples, 2, rows, HD), F32),
            pltpu.VMEM((samples, rows, n_seq), F32),
            pltpu.VMEM((samples, ZS, rows, YS), F32),
            pltpu.VMEM((samples, n_seq, 3, rows, HD), BF16),
            pltpu.VMEM((samples, 4, LEN, HD), BF16),
            pltpu.VMEM((samples, 3, LEN, HD), BF16),
            pltpu.VMEM((LEN, HD), F32),
            pltpu.VMEM((LEN, HD), F32),
            pltpu.VMEM((samples, 8, HD), F32),
            pltpu.VMEM((1, HD), F32),
            pltpu.VMEM((n_dp, 1, HD), F32),
            pltpu.VMEM((1, HD), F32),
            pltpu.VMEM((n_seq, 1, HD), F32),
            dma((samples, n_seq)),
            dma((samples, n_seq)),
            dma((samples, n_seq)),
            dma((samples, n_seq)),
            dma((samples, n_seq)),
            dma((samples, n_seq)),
            dma((n_dp,)),
            dma((n_dp,)),
            dma((n_seq,)),
            dma((n_seq,)),
            dma((3, samples)),
            dma((samples, 3)),
            dma((3,)),
        ],
        compiler_params=pltpu.CompilerParams(
            collective_id=0, has_side_effects=True, vmem_limit_bytes=58 << 20
        ),
    )(q, k, v, targets, scales, frame_ids, freq, bucket_ids)
    out = jax.ShapeDtypeStruct(q.shape, BF16)
    return tuple(
        pl.pallas_call(
            finish,
            out_shape=(out, out, out),
            in_specs=[anywhere] * 3,
            out_specs=(anywhere,) * 3,
            scratch_shapes=[
                pltpu.VMEM(grads.shape, BF16),
                pltpu.VMEM(turns.shape, F32),
                pltpu.VMEM(weighed.shape, F32),
                pltpu.VMEM((3,) + q.shape, BF16),
                dma((samples, n_seq // GROUP)),
                dma((2,)),
                dma((3, samples, n_seq // GROUP)),
            ],
            compiler_params=pltpu.CompilerParams(vmem_limit_bytes=58 << 20),
        )(grads, turns, weighed)
    )


def solution(mesh):
    spec = P("dp", "seq", None)
    return jax.shard_map(
        functools.partial(local, mesh.shape["dp"], mesh.shape["seq"]),
        mesh=mesh,
        in_specs=(spec, spec, spec, spec, spec, P("dp", "seq"), P("dp")),
        out_specs=(spec, spec, spec),
        check_vma=False,
    )
```

```python
import functools
import math

import jax
import jax.numpy as jnp
import numpy as np
from jax import lax
from jax.experimental import pallas as pl
from jax.experimental.pallas import tpu as pltpu
from jax.sharding import PartitionSpec as P

MESH = pl.DeviceIdType.MESH
HD = 128
LEN = 2048
NB = 8
QUARTER = HD // 4
ZS, YS = 8, 4
QB = 256
GROUP = 8
AHEAD = 8
F32 = jnp.float32
BF16 = jnp.bfloat16


def swap_matrix():
    i = lax.broadcasted_iota(jnp.int32, (HD, HD), 0)
    j = lax.broadcasted_iota(jnp.int32, (HD, HD), 1)
    first = (j < QUARTER) & (i == j + QUARTER)
    second = (j >= QUARTER) & (j < 2 * QUARTER) & (i == j - QUARTER)
    return jnp.where(first | second, 1.0, 0.0).astype(BF16)


def turn(blocks, cosine, sine):
    x = jnp.concatenate(blocks, axis=0)
    swapped = jnp.dot(x, swap_matrix(), preferred_element_type=F32)
    shape = (len(blocks),) + blocks[0].shape
    turned = x.astype(F32).reshape(shape) * cosine + swapped.reshape(shape) * sine
    return turned.astype(BF16)


def kernel(
    n_dp,
    n_seq,
    q_ref,
    k_ref,
    v_ref,
    t_ref,
    scale_hbm,
    frame_hbm,
    freq_hbm,
    bucket_ref,
    recv_g,
    turn_hbm,
    weighed_hbm,
    scale_ref,
    frame_ref,
    freq_ref,
    turn_ref,
    weighed_ref,
    held,
    tables,
    upright,
    planes,
    send_in,
    recv_in,
    send_g,
    grad_k,
    grad_v,
    loss_acc,
    loss_mine,
    loss_dp,
    loss_plane,
    loss_seq,
    in_send,
    in_recv,
    t_send,
    t_recv,
    g_send,
    g_recv,
    dp_send,
    dp_recv,
    seq_send,
    seq_recv,
    own_sem,
    load_sem,
    side_sem,
):
    samples, rows, width = q_ref.shape
    last = samples - 1
    dp = lax.axis_index("dp")
    me = lax.axis_index("seq")
    my_z, my_y = me // YS, me % YS

    def partner(i):
        a, dy = i % ZS * 3 % ZS, i // ZS
        half = (a + 1) // 2
        dz = half * (1 - 2 * (a % 2)) + ZS
        return ((my_z + dz) % ZS) * YS + (my_y + dy + half) % YS

    barrier = pltpu.get_barrier_semaphore()

    @pl.loop(1, n_seq)
    def _(i):
        pl.semaphore_signal(barrier, inc=1, device_id=(dp, (me + i) % n_seq), device_id_type=MESH)

    @pl.loop(1, n_dp)
    def _(i):
        pl.semaphore_signal(barrier, inc=1, device_id=((dp + i) % n_dp, me), device_id_type=MESH)

    side = [
        pltpu.make_async_copy(source, there, side_sem.at[i])
        for i, (source, there) in enumerate(
            ((scale_hbm, scale_ref), (frame_hbm, frame_ref), (freq_hbm, freq_ref))
        )
    ]

    def load(s, array):
        source = (q_ref, k_ref, v_ref)[array]
        return pltpu.make_async_copy(source.at[s], held.at[s, array], load_sem.at[s, array])

    for copy in side:
        copy.start()
    for s in range(samples):
        for array in range(3):
            load(s, array).start()

    lane = lax.broadcasted_iota(jnp.int32, (1, HD), 1)
    eye = lax.broadcasted_iota(jnp.int32, (rows, rows), 0) == lax.broadcasted_iota(
        jnp.int32, (rows, rows), 1
    )

    def ready_tables(s):
        ids = frame_ref[s : s + 1, :].astype(F32)
        angle = jnp.sum(jnp.where(eye, ids, 0.0), axis=1, keepdims=True) * freq_ref[...]
        tables[s, 0] = jnp.where(lane < 2 * QUARTER, jnp.cos(angle), 1.0)
        sine = jnp.sin(angle)
        tables[s, 1] = jnp.where(
            lane < QUARTER, -sine, jnp.where(lane < 2 * QUARTER, sine, 0.0)
        )
        columns = jnp.transpose(scale_ref[s])
        upright[s] = columns
        for z in range(ZS):
            planes[s, z] = columns[:, z * YS : (z + 1) * YS]

    def rows_of(device):
        return pl.ds(pl.multiple_of(device * rows, rows), rows)

    def head_of(device):
        return pl.ds(pl.multiple_of(device * HD, HD), HD)

    def in_copy(s, to, source):
        return pltpu.make_async_remote_copy(
            src_ref=send_in.at[s, to],
            dst_ref=recv_in.at[s, pl.ds(0, 3), rows_of(source), :],
            send_sem=in_send.at[s, to],
            recv_sem=in_recv.at[s, source],
            device_id=(dp, to),
            device_id_type=MESH,
        )

    def t_copy(s, to, source):
        return pltpu.make_async_remote_copy(
            src_ref=t_ref.at[s, :, head_of(to)],
            dst_ref=recv_in.at[s, 3, rows_of(source), :],
            send_sem=t_send.at[s, to],
            recv_sem=t_recv.at[s, source],
            device_id=(dp, to),
            device_id_type=MESH,
        )

    def in_own(s):
        return pltpu.make_async_copy(
            send_in.at[s, me], recv_in.at[s, pl.ds(0, 3), rows_of(me), :], own_sem.at[0, s]
        )

    def t_own(s):
        return pltpu.make_async_copy(
            t_ref.at[s, :, head_of(me)], recv_in.at[s, 3, rows_of(me), :], own_sem.at[2, s]
        )

    def wait_in(s):
        @pl.loop(1, n_seq)
        def _(i):
            source = (me + i) % n_seq
            t_copy(s, source, source).wait_recv()
            in_copy(s, source, source).wait_recv()

        in_own(s).wait()
        t_own(s).wait()

    def g_copy(s, i):
        to = partner(i)
        return pltpu.make_async_remote_copy(
            src_ref=send_g.at[s, :, pl.ds(pl.multiple_of(to * rows, rows), rows), :],
            dst_ref=recv_g.at[s, me],
            send_sem=g_send.at[s, i],
            recv_sem=g_recv.at[s, me],
            device_id=(dp, to),
            device_id_type=MESH,
        )

    def g_own(s):
        return pltpu.make_async_copy(
            send_g.at[s, :, pl.ds(pl.multiple_of(me * rows, rows), rows), :],
            recv_g.at[s, me],
            own_sem.at[1, s],
        )

    def prepare(s, z):
        def block(array, y):
            return held[s, array, :, pl.ds(pl.multiple_of((z * YS + y) * HD, HD), HD)]

        turned = turn(
            [block(array, y) for array in range(2) for y in range(YS)], tables[s, 0], tables[s, 1]
        )
        scales = planes[s, z]
        for y in range(YS):
            head = z * YS + y
            send_in[s, head, 0] = turned[y]
            send_in[s, head, 1] = turned[YS + y]
            send_in[s, head, 2] = (block(2, y).astype(F32) * scales[:, y : y + 1]).astype(BF16)

    def attend(s):
        grad_k[...] = jnp.zeros_like(grad_k)
        grad_v[...] = jnp.zeros_like(grad_v)
        loss_acc[s] = jnp.zeros_like(loss_acc[s])

        @pl.loop(0, LEN // QB)
        def _(b):
            block = pl.ds(pl.multiple_of(b * QB, QB), QB)
            q = recv_in[s, 0, block]
            k = recv_in[s, 1]
            v = recv_in[s, 2]
            scores = lax.dot_general(q, k, (((1,), (1,)), ((), ())), preferred_element_type=F32)
            top = jnp.max(scores, axis=1, keepdims=True)
            e = jnp.exp2((scores - top) * (HD**-0.5 * math.log2(math.e)))
            p = e * (1.0 / jnp.sum(e, axis=1, keepdims=True))
            p_low = p.astype(BF16)
            attended = jnp.dot(p_low, v, preferred_element_type=F32).astype(BF16).astype(F32)
            errors = attended - recv_in[s, 3, block].astype(F32)
            loss_acc[s] += jnp.sum((errors * errors).reshape(QB // 8, 8, HD), axis=0)
            cotangent = errors.astype(BF16)
            delta = jnp.sum(cotangent.astype(F32) * attended, axis=1, keepdims=True)
            grad_v[...] += lax.dot_general(
                p_low, cotangent, (((0,), (0,)), ((), ())), preferred_element_type=F32
            )
            grad_p = lax.dot_general(
                cotangent, v, (((1,), (1,)), ((), ())), preferred_element_type=F32
            )
            grad_s = (p * (grad_p - delta) * HD**-0.5).astype(BF16)
            send_g[s, 0, block] = jnp.dot(grad_s, k, preferred_element_type=F32).astype(BF16)
            grad_k[...] += lax.dot_general(
                grad_s, q, (((0,), (0,)), ((), ())), preferred_element_type=F32
            )

        send_g[s, 1] = grad_k[...].astype(BF16)
        send_g[s, 2] = grad_v[...].astype(BF16)

    def start_g(s, begin, end):
        @pl.loop(begin, end)
        def _(j):
            g_copy(s, n_seq - j).start()

    pl.semaphore_wait(barrier, n_seq + n_dp - 2)

    @pl.loop(1, n_seq)
    def _(j):
        t_copy(0, partner(n_seq - j), me).start()

    for copy in side:
        copy.wait()
    for s in range(samples):
        ready_tables(s)
        t_own(s).start()
        for array in range(3):
            load(s, array).wait()

        @pl.loop(0, ZS)
        def _(z):
            prepare(s, z)

        if s == 0:

            @pl.loop(1, n_seq)
            def _(j):
                in_copy(s, partner(n_seq - j), me).start()

        else:

            @pl.loop(1, n_seq)
            def _(j):
                to = partner(n_seq - j)
                in_copy(s - 1, to, me).wait_send()
                t_copy(s, to, me).start()
                in_copy(s, to, me).start()

        in_own(s).start()

    @pl.loop(0, samples)
    def _(s):
        wait_in(s)
        attend(s)

        @pl.when(s < last)
        def _():
            start_g(s, 1, AHEAD + 1)

            @pl.loop(1, n_seq - AHEAD)
            def _(j):
                in_copy(last, partner(n_seq - j), me).wait_send()
                g_copy(s, n_seq - AHEAD - j).start()

            @pl.loop(n_seq - AHEAD, n_seq)
            def _(j):
                in_copy(last, partner(n_seq - j), me).wait_send()

            g_own(s).start()

    mine = jnp.zeros((1, HD), F32)
    for s in range(samples):
        bucket = bucket_ref[s]
        total = jnp.sum(jnp.sum(loss_acc[s], axis=0, keepdims=True), axis=1, keepdims=True)
        mine += jnp.where(lane == bucket, total / (LEN * width), 0.0)
        mine += jnp.where(lane == bucket + NB, 1.0 / n_seq, 0.0)
    loss_mine[...] = mine

    def dp_copy(i):
        to = (dp + i) % n_dp
        return pltpu.make_async_remote_copy(
            src_ref=loss_mine,
            dst_ref=loss_dp.at[dp],
            send_sem=dp_send.at[i],
            recv_sem=dp_recv.at[dp],
            device_id=(to, me),
            device_id_type=MESH,
        )

    def seq_copy(i):
        to = (me + i) % n_seq
        return pltpu.make_async_remote_copy(
            src_ref=loss_plane,
            dst_ref=loss_seq.at[me],
            send_sem=seq_send.at[i],
            recv_sem=seq_recv.at[me],
            device_id=(dp, to),
            device_id_type=MESH,
        )

    @pl.loop(1, n_dp)
    def _(i):
        dp_copy(i).start()

    loss_dp[dp] = mine
    start_g(last, 1, 2 * n_seq // 3)
    g_own(last).start()

    @pl.loop(1, n_dp)
    def _(i):
        src = (dp + i) % n_dp
        pltpu.make_async_remote_copy(
            src_ref=loss_mine,
            dst_ref=loss_dp.at[src],
            send_sem=dp_send.at[i],
            recv_sem=dp_recv.at[src],
            device_id=(src, me),
            device_id_type=MESH,
        ).wait_recv()

    plane_loss = jnp.sum(loss_dp[...], axis=0)
    loss_plane[...] = plane_loss

    @pl.loop(1, n_seq)
    def _(i):
        seq_copy(i).start()

    loss_seq[me] = plane_loss
    start_g(last, 2 * n_seq // 3, n_seq)

    @pl.loop(1, n_seq)
    def _(i):
        src = (me + i) % n_seq
        pltpu.make_async_remote_copy(
            src_ref=loss_plane,
            dst_ref=loss_seq.at[src],
            send_sem=seq_send.at[i],
            recv_sem=seq_recv.at[src],
            device_id=(dp, src),
            device_id_type=MESH,
        ).wait_recv()

    buckets = jnp.sum(loss_seq[...], axis=0)
    sum_loss = jnp.sum(jnp.where(lane < NB, buckets, 0.0), axis=1, keepdims=True)
    sum_count = jnp.sum(
        jnp.where((lane >= NB) & (lane < 2 * NB), buckets, 0.0), axis=1, keepdims=True
    )
    mean_all = sum_loss / sum_count

    for s in range(samples):
        bucket = bucket_ref[s]
        chosen_loss = jnp.sum(jnp.where(lane == bucket, buckets, 0.0), axis=1, keepdims=True)
        chosen_count = jnp.sum(
            jnp.where(lane == bucket + NB, buckets, 0.0), axis=1, keepdims=True
        )
        weight = mean_all / (chosen_loss / chosen_count + 1e-5)
        turn_ref[s, 0] = weight * tables[s, 0]
        turn_ref[s, 1] = -weight * tables[s, 1]
        weighed = weight * upright[s]
        for g in range(n_seq // GROUP):
            weighed_ref[s, g] = weighed[:, g * GROUP : (g + 1) * GROUP]

    results = (
        pltpu.make_async_copy(turn_ref, turn_hbm, side_sem.at[0]),
        pltpu.make_async_copy(weighed_ref, weighed_hbm, side_sem.at[1]),
    )
    for copy in results:
        copy.start()

    for s in range(samples):
        g_own(s).wait()

        @pl.loop(1, n_seq)
        def _(i):
            src = (me + i) % n_seq
            pltpu.make_async_remote_copy(
                src_ref=send_g.at[s, :, pl.ds(pl.multiple_of(src * rows, rows), rows), :],
                dst_ref=recv_g.at[s, src],
                send_sem=g_send.at[s, i],
                recv_sem=g_recv.at[s, src],
                device_id=(dp, src),
                device_id_type=MESH,
            ).wait_recv()

    @pl.loop(1, n_seq)
    def _(i):
        for s in range(samples):
            g_copy(s, i).wait_send()
            t_copy(s, (me + i) % n_seq, me).wait_send()
        seq_copy(i).wait_send()

    @pl.loop(1, n_dp)
    def _(i):
        dp_copy(i).wait_send()

    for copy in results:
        copy.wait()


def finish(
    grad_hbm,
    turn_hbm,
    weighed_hbm,
    oq_hbm,
    ok_hbm,
    ov_hbm,
    grad_ref,
    turn_ref,
    weighed_ref,
    out_ref,
    grad_sem,
    side_sem,
    out_sem,
):
    samples, heads = grad_ref.shape[:2]
    groups = heads // GROUP

    def load(s, g):
        some = pl.ds(g * GROUP, GROUP)
        return pltpu.make_async_copy(
            grad_hbm.at[s, some], grad_ref.at[s, some], grad_sem.at[s, g]
        )

    def store(s, g, array):
        some = pl.ds(pl.multiple_of(g * (GROUP * HD), GROUP * HD), GROUP * HD)
        return pltpu.make_async_copy(
            out_ref.at[array, s, :, some],
            (oq_hbm, ok_hbm, ov_hbm)[array].at[s, :, some],
            out_sem.at[array, s, g],
        )

    side = (
        pltpu.make_async_copy(turn_hbm, turn_ref, side_sem.at[0]),
        pltpu.make_async_copy(weighed_hbm, weighed_ref, side_sem.at[1]),
    )
    for copy in side:
        copy.start()

    @pl.loop(0, samples * groups)
    def _(i):
        load(i // groups, i % groups).start()

    for copy in side:
        copy.wait()

    @pl.loop(0, samples * groups)
    def _(i):
        s, g = i // groups, i % groups
        load(s, g).wait()

        def columns(h):
            return pl.ds(pl.multiple_of((g * GROUP + h) * HD, HD), HD)

        turned = turn(
            [grad_ref[s, g * GROUP + h, array] for array in range(2) for h in range(GROUP)],
            turn_ref[s, 0],
            turn_ref[s, 1],
        )
        for array in range(2):
            for h in range(GROUP):
                out_ref[array, s, :, columns(h)] = turned[array * GROUP + h]
            store(s, g, array).start()
        scales = weighed_ref[s, g]
        for h in range(GROUP):
            out_ref[2, s, :, columns(h)] = (
                grad_ref[s, g * GROUP + h, 2].astype(F32) * scales[:, h : h + 1]
            ).astype(BF16)
        store(s, g, 2).start()

    @pl.loop(0, samples * groups)
    def _(i):
        for array in range(3):
            store(i // groups, i % groups, array).wait()


def local(n_dp, n_seq, q, k, v, scales, targets, frame_ids, bucket_ids):
    samples, rows, width = q.shape
    exponent = np.arange(HD) % QUARTER / QUARTER
    freq = np.where(np.arange(HD) < 2 * QUARTER, 10000.0 ** (-exponent), 0.0)
    freq = jnp.asarray(freq[None, :], F32)
    scales = jnp.swapaxes(scales, 1, 2)
    smem = pl.BlockSpec(memory_space=pltpu.SMEM)
    anywhere = pl.BlockSpec(memory_space=pl.ANY)
    dma = pltpu.SemaphoreType.DMA
    grads, turns, weighed = pl.pallas_call(
        functools.partial(kernel, n_dp, n_seq),
        out_shape=(
            jax.ShapeDtypeStruct((samples, n_seq, 3, rows, HD), BF16),
            jax.ShapeDtypeStruct((samples, 2, rows, HD), F32),
            jax.ShapeDtypeStruct((samples, n_seq // GROUP, rows, GROUP), F32),
        ),
        in_specs=[anywhere] * 7 + [smem],
        out_specs=(anywhere, anywhere, anywhere),
        scratch_shapes=[
            pltpu.VMEM(scales.shape, F32),
            pltpu.VMEM(frame_ids.shape, jnp.int32),
            pltpu.VMEM(freq.shape, F32),
            pltpu.VMEM((samples, 2, rows, HD), F32),
            pltpu.VMEM((samples, n_seq // GROUP, rows, GROUP), F32),
            pltpu.VMEM((samples, 3, rows, width), BF16),
            pltpu.VMEM((samples, 2, rows, HD), F32),
            pltpu.VMEM((samples, rows, n_seq), F32),
            pltpu.VMEM((samples, ZS, rows, YS), F32),
            pltpu.VMEM((samples, n_seq, 3, rows, HD), BF16),
            pltpu.VMEM((samples, 4, LEN, HD), BF16),
            pltpu.VMEM((samples, 3, LEN, HD), BF16),
            pltpu.VMEM((LEN, HD), F32),
            pltpu.VMEM((LEN, HD), F32),
            pltpu.VMEM((samples, 8, HD), F32),
            pltpu.VMEM((1, HD), F32),
            pltpu.VMEM((n_dp, 1, HD), F32),
            pltpu.VMEM((1, HD), F32),
            pltpu.VMEM((n_seq, 1, HD), F32),
            dma((samples, n_seq)),
            dma((samples, n_seq)),
            dma((samples, n_seq)),
            dma((samples, n_seq)),
            dma((samples, n_seq)),
            dma((samples, n_seq)),
            dma((n_dp,)),
            dma((n_dp,)),
            dma((n_seq,)),
            dma((n_seq,)),
            dma((3, samples)),
            dma((samples, 3)),
            dma((3,)),
        ],
        compiler_params=pltpu.CompilerParams(
            collective_id=0, has_side_effects=True, vmem_limit_bytes=58 << 20
        ),
    )(q, k, v, targets, scales, frame_ids, freq, bucket_ids)
    out = jax.ShapeDtypeStruct(q.shape, BF16)
    return tuple(
        pl.pallas_call(
            finish,
            out_shape=(out, out, out),
            in_specs=[anywhere] * 3,
            out_specs=(anywhere,) * 3,
            scratch_shapes=[
                pltpu.VMEM(grads.shape, BF16),
                pltpu.VMEM(turns.shape, F32),
                pltpu.VMEM(weighed.shape, F32),
                pltpu.VMEM((3,) + q.shape, BF16),
                dma((samples, n_seq // GROUP)),
                dma((2,)),
                dma((3, samples, n_seq // GROUP)),
            ],
            compiler_params=pltpu.CompilerParams(vmem_limit_bytes=58 << 20),
        )(grads, turns, weighed)
    )


def solution(mesh):
    spec = P("dp", "seq", None)
    return jax.shard_map(
        functools.partial(local, mesh.shape["dp"], mesh.shape["seq"]),
        mesh=mesh,
        in_specs=(spec, spec, spec, spec, spec, P("dp", "seq"), P("dp")),
        out_specs=(spec, spec, spec),
        check_vma=False,
    )
```

```python
import functools
import math

import jax
import jax.numpy as jnp
import numpy as np
from jax import lax
from jax.experimental import pallas as pl
from jax.experimental.pallas import tpu as pltpu
from jax.sharding import PartitionSpec as P

MESH = pl.DeviceIdType.MESH
HD = 128
LEN = 2048
NB = 8
QUARTER = HD // 4
ZS, YS = 8, 4
QB = 256
GROUP = 8
AHEAD = 8
F32 = jnp.float32
BF16 = jnp.bfloat16


def swap_matrix():
    i = lax.broadcasted_iota(jnp.int32, (HD, HD), 0)
    j = lax.broadcasted_iota(jnp.int32, (HD, HD), 1)
    first = (j < QUARTER) & (i == j + QUARTER)
    second = (j >= QUARTER) & (j < 2 * QUARTER) & (i == j - QUARTER)
    return jnp.where(first | second, 1.0, 0.0).astype(BF16)


def turn(blocks, cosine, sine):
    x = jnp.concatenate(blocks, axis=0)
    swapped = jnp.dot(x, swap_matrix(), preferred_element_type=F32)
    shape = (len(blocks),) + blocks[0].shape
    turned = x.astype(F32).reshape(shape) * cosine + swapped.reshape(shape) * sine
    return turned.astype(BF16)


def turn_back(grad_ref, g, tables, scales, out_ref):
    turned = turn(
        [grad_ref[g * GROUP + h, array] for array in range(2) for h in range(GROUP)], *tables
    )
    for h in range(GROUP):
        columns = pl.ds(pl.multiple_of((g * GROUP + h) * HD, HD), HD)
        for array in range(2):
            out_ref[array, :, columns] = turned[array * GROUP + h]
        out_ref[2, :, columns] = (
            grad_ref[g * GROUP + h, 2].astype(F32) * scales[:, h : h + 1]
        ).astype(BF16)


def kernel(
    n_dp,
    n_seq,
    q_ref,
    k_ref,
    v_ref,
    t_ref,
    scale_hbm,
    frame_hbm,
    freq_hbm,
    bucket_ref,
    recv_g,
    turn_hbm,
    weighed_hbm,
    done_hbm,
    scale_ref,
    frame_ref,
    freq_ref,
    turn_ref,
    weighed_ref,
    first_g,
    done_ref,
    held,
    tables,
    upright,
    planes,
    send_in,
    recv_in,
    send_g,
    grad_k,
    grad_v,
    loss_acc,
    loss_mine,
    loss_dp,
    loss_plane,
    loss_seq,
    in_send,
    in_recv,
    t_send,
    t_recv,
    g_send,
    g_recv,
    dp_send,
    dp_recv,
    seq_send,
    seq_recv,
    own_sem,
    load_sem,
    side_sem,
):
    samples, rows, width = q_ref.shape
    last = samples - 1
    dp = lax.axis_index("dp")
    me = lax.axis_index("seq")
    my_z, my_y = me // YS, me % YS

    def partner(i):
        a, dy = i % ZS * 3 % ZS, i // ZS
        half = (a + 1) // 2
        dz = half * (1 - 2 * (a % 2)) + ZS
        return ((my_z + dz) % ZS) * YS + (my_y + dy + half) % YS

    barrier = pltpu.get_barrier_semaphore()

    @pl.loop(1, n_seq)
    def _(i):
        pl.semaphore_signal(barrier, inc=1, device_id=(dp, (me + i) % n_seq), device_id_type=MESH)

    @pl.loop(1, n_dp)
    def _(i):
        pl.semaphore_signal(barrier, inc=1, device_id=((dp + i) % n_dp, me), device_id_type=MESH)

    side = [
        pltpu.make_async_copy(source, there, side_sem.at[i])
        for i, (source, there) in enumerate(
            ((scale_hbm, scale_ref), (frame_hbm, frame_ref), (freq_hbm, freq_ref))
        )
    ]

    def load(s, array):
        source = (q_ref, k_ref, v_ref)[array]
        return pltpu.make_async_copy(source.at[s], held.at[s, array], load_sem.at[s, array])

    for copy in side:
        copy.start()
    for s in range(samples):
        for array in range(3):
            load(s, array).start()

    lane = lax.broadcasted_iota(jnp.int32, (1, HD), 1)
    eye = lax.broadcasted_iota(jnp.int32, (rows, rows), 0) == lax.broadcasted_iota(
        jnp.int32, (rows, rows), 1
    )

    def ready_tables(s):
        ids = frame_ref[s : s + 1, :].astype(F32)
        angle = jnp.sum(jnp.where(eye, ids, 0.0), axis=1, keepdims=True) * freq_ref[...]
        tables[s, 0] = jnp.where(lane < 2 * QUARTER, jnp.cos(angle), 1.0)
        sine = jnp.sin(angle)
        tables[s, 1] = jnp.where(
            lane < QUARTER, -sine, jnp.where(lane < 2 * QUARTER, sine, 0.0)
        )
        columns = jnp.transpose(scale_ref[s])
        upright[s] = columns
        for z in range(ZS):
            planes[s, z] = columns[:, z * YS : (z + 1) * YS]

    def rows_of(device):
        return pl.ds(pl.multiple_of(device * rows, rows), rows)

    def head_of(device):
        return pl.ds(pl.multiple_of(device * HD, HD), HD)

    def in_copy(s, to, source):
        return pltpu.make_async_remote_copy(
            src_ref=send_in.at[s, to],
            dst_ref=recv_in.at[s, pl.ds(0, 3), rows_of(source), :],
            send_sem=in_send.at[s, to],
            recv_sem=in_recv.at[s, source],
            device_id=(dp, to),
            device_id_type=MESH,
        )

    def t_copy(s, to, source):
        return pltpu.make_async_remote_copy(
            src_ref=t_ref.at[s, :, head_of(to)],
            dst_ref=recv_in.at[s, 3, rows_of(source), :],
            send_sem=t_send.at[s, to],
            recv_sem=t_recv.at[s, source],
            device_id=(dp, to),
            device_id_type=MESH,
        )

    def in_own(s):
        return pltpu.make_async_copy(
            send_in.at[s, me], recv_in.at[s, pl.ds(0, 3), rows_of(me), :], own_sem.at[0, s]
        )

    def t_own(s):
        return pltpu.make_async_copy(
            t_ref.at[s, :, head_of(me)], recv_in.at[s, 3, rows_of(me), :], own_sem.at[2, s]
        )

    def wait_in(s):
        @pl.loop(1, n_seq)
        def _(i):
            source = (me + i) % n_seq
            t_copy(s, source, source).wait_recv()
            in_copy(s, source, source).wait_recv()

        in_own(s).wait()
        t_own(s).wait()

    def g_copy(s, i):
        to = partner(i)
        return pltpu.make_async_remote_copy(
            src_ref=send_g.at[s, :, pl.ds(pl.multiple_of(to * rows, rows), rows), :],
            dst_ref=(recv_g if s == last else first_g).at[me],
            send_sem=g_send.at[s, i],
            recv_sem=g_recv.at[s, me],
            device_id=(dp, to),
            device_id_type=MESH,
        )

    def g_own(s):
        return pltpu.make_async_copy(
            send_g.at[s, :, pl.ds(pl.multiple_of(me * rows, rows), rows), :],
            (recv_g if s == last else first_g).at[me],
            own_sem.at[1, s],
        )

    def prepare(s, z):
        def block(array, y):
            return held[s, array, :, pl.ds(pl.multiple_of((z * YS + y) * HD, HD), HD)]

        turned = turn(
            [block(array, y) for array in range(2) for y in range(YS)], tables[s, 0], tables[s, 1]
        )
        scales = planes[s, z]
        for y in range(YS):
            head = z * YS + y
            send_in[s, head, 0] = turned[y]
            send_in[s, head, 1] = turned[YS + y]
            send_in[s, head, 2] = (block(2, y).astype(F32) * scales[:, y : y + 1]).astype(BF16)

    def attend(s):
        grad_k[...] = jnp.zeros_like(grad_k)
        grad_v[...] = jnp.zeros_like(grad_v)
        loss_acc[s] = jnp.zeros_like(loss_acc[s])

        @pl.loop(0, LEN // QB)
        def _(b):
            block = pl.ds(pl.multiple_of(b * QB, QB), QB)
            q = recv_in[s, 0, block]
            k = recv_in[s, 1]
            v = recv_in[s, 2]
            scores = lax.dot_general(q, k, (((1,), (1,)), ((), ())), preferred_element_type=F32)
            top = jnp.max(scores, axis=1, keepdims=True)
            e = jnp.exp2((scores - top) * (HD**-0.5 * math.log2(math.e)))
            p = e * (1.0 / jnp.sum(e, axis=1, keepdims=True))
            p_low = p.astype(BF16)
            attended = jnp.dot(p_low, v, preferred_element_type=F32).astype(BF16).astype(F32)
            errors = attended - recv_in[s, 3, block].astype(F32)
            loss_acc[s] += jnp.sum((errors * errors).reshape(QB // 8, 8, HD), axis=0)
            cotangent = errors.astype(BF16)
            delta = jnp.sum(cotangent.astype(F32) * attended, axis=1, keepdims=True)
            grad_v[...] += lax.dot_general(
                p_low, cotangent, (((0,), (0,)), ((), ())), preferred_element_type=F32
            )
            grad_p = lax.dot_general(
                cotangent, v, (((1,), (1,)), ((), ())), preferred_element_type=F32
            )
            grad_s = (p * (grad_p - delta) * HD**-0.5).astype(BF16)
            send_g[s, 0, block] = jnp.dot(grad_s, k, preferred_element_type=F32).astype(BF16)
            grad_k[...] += lax.dot_general(
                grad_s, q, (((0,), (0,)), ((), ())), preferred_element_type=F32
            )

        send_g[s, 1] = grad_k[...].astype(BF16)
        send_g[s, 2] = grad_v[...].astype(BF16)

    def start_g(s, begin, end):
        @pl.loop(begin, end)
        def _(j):
            g_copy(s, n_seq - j).start()

    pl.semaphore_wait(barrier, n_seq + n_dp - 2)

    @pl.loop(1, n_seq)
    def _(j):
        t_copy(0, partner(n_seq - j), me).start()

    for copy in side:
        copy.wait()
    for s in range(samples):
        ready_tables(s)
        t_own(s).start()
        for array in range(3):
            load(s, array).wait()

        @pl.loop(0, ZS)
        def _(z):
            prepare(s, z)

        if s == 0:

            @pl.loop(1, n_seq)
            def _(j):
                in_copy(s, partner(n_seq - j), me).start()

        else:

            @pl.loop(1, n_seq)
            def _(j):
                to = partner(n_seq - j)
                in_copy(s - 1, to, me).wait_send()
                t_copy(s, to, me).start()
                in_copy(s, to, me).start()

        in_own(s).start()

    @pl.loop(0, samples)
    def _(s):
        wait_in(s)
        attend(s)

        @pl.when(s < last)
        def _():
            start_g(0, 1, AHEAD + 1)

            @pl.loop(1, n_seq - AHEAD)
            def _(j):
                in_copy(last, partner(n_seq - j), me).wait_send()
                g_copy(0, n_seq - AHEAD - j).start()

            @pl.loop(n_seq - AHEAD, n_seq)
            def _(j):
                in_copy(last, partner(n_seq - j), me).wait_send()

            g_own(0).start()

    mine = jnp.zeros((1, HD), F32)
    for s in range(samples):
        bucket = bucket_ref[s]
        total = jnp.sum(jnp.sum(loss_acc[s], axis=0, keepdims=True), axis=1, keepdims=True)
        mine += jnp.where(lane == bucket, total / (LEN * width), 0.0)
        mine += jnp.where(lane == bucket + NB, 1.0 / n_seq, 0.0)
    loss_mine[...] = mine

    def dp_copy(i):
        to = (dp + i) % n_dp
        return pltpu.make_async_remote_copy(
            src_ref=loss_mine,
            dst_ref=loss_dp.at[dp],
            send_sem=dp_send.at[i],
            recv_sem=dp_recv.at[dp],
            device_id=(to, me),
            device_id_type=MESH,
        )

    def seq_copy(i):
        to = (me + i) % n_seq
        return pltpu.make_async_remote_copy(
            src_ref=loss_plane,
            dst_ref=loss_seq.at[me],
            send_sem=seq_send.at[i],
            recv_sem=seq_recv.at[me],
            device_id=(dp, to),
            device_id_type=MESH,
        )

    @pl.loop(1, n_dp)
    def _(i):
        dp_copy(i).start()

    loss_dp[dp] = mine
    start_g(last, 1, 2 * n_seq // 3)
    g_own(last).start()

    @pl.loop(1, n_dp)
    def _(i):
        src = (dp + i) % n_dp
        pltpu.make_async_remote_copy(
            src_ref=loss_mine,
            dst_ref=loss_dp.at[src],
            send_sem=dp_send.at[i],
            recv_sem=dp_recv.at[src],
            device_id=(src, me),
            device_id_type=MESH,
        ).wait_recv()

    plane_loss = jnp.sum(loss_dp[...], axis=0)
    loss_plane[...] = plane_loss

    @pl.loop(1, n_seq)
    def _(i):
        seq_copy(i).start()

    loss_seq[me] = plane_loss
    start_g(last, 2 * n_seq // 3, n_seq)

    @pl.loop(1, n_seq)
    def _(i):
        src = (me + i) % n_seq
        pltpu.make_async_remote_copy(
            src_ref=loss_plane,
            dst_ref=loss_seq.at[src],
            send_sem=seq_send.at[i],
            recv_sem=seq_recv.at[src],
            device_id=(dp, src),
            device_id_type=MESH,
        ).wait_recv()

    buckets = jnp.sum(loss_seq[...], axis=0)
    sum_loss = jnp.sum(jnp.where(lane < NB, buckets, 0.0), axis=1, keepdims=True)
    sum_count = jnp.sum(
        jnp.where((lane >= NB) & (lane < 2 * NB), buckets, 0.0), axis=1, keepdims=True
    )
    mean_all = sum_loss / sum_count

    for s in range(samples):
        bucket = bucket_ref[s]
        chosen_loss = jnp.sum(jnp.where(lane == bucket, buckets, 0.0), axis=1, keepdims=True)
        chosen_count = jnp.sum(
            jnp.where(lane == bucket + NB, buckets, 0.0), axis=1, keepdims=True
        )
        weight = mean_all / (chosen_loss / chosen_count + 1e-5)
        turn_ref[s, 0] = weight * tables[s, 0]
        turn_ref[s, 1] = -weight * tables[s, 1]
        weighed = weight * upright[s]
        for g in range(n_seq // GROUP):
            weighed_ref[s, g] = weighed[:, g * GROUP : (g + 1) * GROUP]

    results = (
        pltpu.make_async_copy(turn_ref.at[last], turn_hbm, side_sem.at[0]),
        pltpu.make_async_copy(weighed_ref.at[last], weighed_hbm, side_sem.at[1]),
    )
    for copy in results:
        copy.start()

    for s in range(samples):
        g_own(s).wait()

        @pl.loop(1, n_seq)
        def _(i):
            src = (me + i) % n_seq
            pltpu.make_async_remote_copy(
                src_ref=send_g.at[s, :, pl.ds(pl.multiple_of(src * rows, rows), rows), :],
                dst_ref=(recv_g if s == last else first_g).at[src],
                send_sem=g_send.at[s, i],
                recv_sem=g_recv.at[s, src],
                device_id=(dp, src),
                device_id_type=MESH,
            ).wait_recv()

        if s == 0:

            @pl.loop(0, n_seq // GROUP)
            def _(g):
                turn_back(
                    first_g, g, (turn_ref[0, 0], turn_ref[0, 1]), weighed_ref[0, g], done_ref
                )

            done = pltpu.make_async_copy(done_ref, done_hbm, side_sem.at[2])
            done.start()

    @pl.loop(1, n_seq)
    def _(i):
        for s in range(samples):
            g_copy(s, i).wait_send()
            t_copy(s, (me + i) % n_seq, me).wait_send()
        seq_copy(i).wait_send()

    @pl.loop(1, n_dp)
    def _(i):
        dp_copy(i).wait_send()

    for copy in (*results, done):
        copy.wait()


def finish(
    grad_hbm,
    turn_hbm,
    weighed_hbm,
    done_hbm,
    oq_hbm,
    ok_hbm,
    ov_hbm,
    grad_ref,
    turn_ref,
    weighed_ref,
    out_ref,
    done_ref,
    grad_sem,
    side_sem,
    out_sem,
    done_sem,
):
    groups = grad_ref.shape[0] // GROUP
    last = oq_hbm.shape[0] - 1
    outs = (oq_hbm, ok_hbm, ov_hbm)

    def load(g):
        some = pl.ds(g * GROUP, GROUP)
        return pltpu.make_async_copy(grad_hbm.at[some], grad_ref.at[some], grad_sem.at[g])

    def store(g, array):
        some = pl.ds(pl.multiple_of(g * (GROUP * HD), GROUP * HD), GROUP * HD)
        return pltpu.make_async_copy(
            out_ref.at[array, :, some], outs[array].at[last, :, some], out_sem.at[array, g]
        )

    side = (
        pltpu.make_async_copy(turn_hbm, turn_ref, side_sem.at[0]),
        pltpu.make_async_copy(weighed_hbm, weighed_ref, side_sem.at[1]),
    )
    done_in = [
        pltpu.make_async_copy(done_hbm.at[array], done_ref.at[array], done_sem.at[0, array])
        for array in range(3)
    ]
    done_out = [
        pltpu.make_async_copy(done_ref.at[array], outs[array].at[0], done_sem.at[1, array])
        for array in range(3)
    ]
    load(0).start()
    for copy in side:
        copy.start()

    @pl.loop(1, groups)
    def _(g):
        load(g).start()

    for copy in done_in:
        copy.start()
    for copy in side:
        copy.wait()

    @pl.loop(0, groups)
    def _(g):
        load(g).wait()
        turn_back(grad_ref, g, (turn_ref[0], turn_ref[1]), weighed_ref[g], out_ref)
        for array in range(3):
            store(g, array).start()

        @pl.when(g == 0)
        def _():
            for array in range(3):
                done_in[array].wait()
                done_out[array].start()

    @pl.loop(0, groups)
    def _(g):
        for array in range(3):
            store(g, array).wait()

    for copy in done_out:
        copy.wait()


def local(n_dp, n_seq, q, k, v, scales, targets, frame_ids, bucket_ids):
    samples, rows, width = q.shape
    exponent = np.arange(HD) % QUARTER / QUARTER
    freq = np.where(np.arange(HD) < 2 * QUARTER, 10000.0 ** (-exponent), 0.0)
    freq = jnp.asarray(freq[None, :], F32)
    scales = jnp.swapaxes(scales, 1, 2)
    smem = pl.BlockSpec(memory_space=pltpu.SMEM)
    anywhere = pl.BlockSpec(memory_space=pl.ANY)
    dma = pltpu.SemaphoreType.DMA
    grads, turns, weighed, done = pl.pallas_call(
        functools.partial(kernel, n_dp, n_seq),
        out_shape=(
            jax.ShapeDtypeStruct((n_seq, 3, rows, HD), BF16),
            jax.ShapeDtypeStruct((2, rows, HD), F32),
            jax.ShapeDtypeStruct((n_seq // GROUP, rows, GROUP), F32),
            jax.ShapeDtypeStruct((3, rows, width), BF16),
        ),
        in_specs=[anywhere] * 7 + [smem],
        out_specs=(anywhere,) * 4,
        scratch_shapes=[
            pltpu.VMEM(scales.shape, F32),
            pltpu.VMEM(frame_ids.shape, jnp.int32),
            pltpu.VMEM(freq.shape, F32),
            pltpu.VMEM((samples, 2, rows, HD), F32),
            pltpu.VMEM((samples, n_seq // GROUP, rows, GROUP), F32),
            pltpu.VMEM((n_seq, 3, rows, HD), BF16),
            pltpu.VMEM((3, rows, width), BF16),
            pltpu.VMEM((samples, 3, rows, width), BF16),
            pltpu.VMEM((samples, 2, rows, HD), F32),
            pltpu.VMEM((samples, rows, n_seq), F32),
            pltpu.VMEM((samples, ZS, rows, YS), F32),
            pltpu.VMEM((samples, n_seq, 3, rows, HD), BF16),
            pltpu.VMEM((samples, 4, LEN, HD), BF16),
            pltpu.VMEM((samples, 3, LEN, HD), BF16),
            pltpu.VMEM((LEN, HD), F32),
            pltpu.VMEM((LEN, HD), F32),
            pltpu.VMEM((samples, 8, HD), F32),
            pltpu.VMEM((1, HD), F32),
            pltpu.VMEM((n_dp, 1, HD), F32),
            pltpu.VMEM((1, HD), F32),
            pltpu.VMEM((n_seq, 1, HD), F32),
            dma((samples, n_seq)),
            dma((samples, n_seq)),
            dma((samples, n_seq)),
            dma((samples, n_seq)),
            dma((samples, n_seq)),
            dma((samples, n_seq)),
            dma((n_dp,)),
            dma((n_dp,)),
            dma((n_seq,)),
            dma((n_seq,)),
            dma((3, samples)),
            dma((samples, 3)),
            dma((3,)),
        ],
        compiler_params=pltpu.CompilerParams(
            collective_id=0, has_side_effects=True, vmem_limit_bytes=58 << 20
        ),
    )(q, k, v, targets, scales, frame_ids, freq, bucket_ids)
    out = jax.ShapeDtypeStruct(q.shape, BF16)
    return tuple(
        pl.pallas_call(
            finish,
            out_shape=(out, out, out),
            in_specs=[anywhere] * 4,
            out_specs=(anywhere,) * 3,
            scratch_shapes=[
                pltpu.VMEM(grads.shape, BF16),
                pltpu.VMEM(turns.shape, F32),
                pltpu.VMEM(weighed.shape, F32),
                pltpu.VMEM(done.shape, BF16),
                pltpu.VMEM(done.shape, BF16),
                dma((n_seq // GROUP,)),
                dma((2,)),
                dma((3, n_seq // GROUP)),
                dma((2, 3)),
            ],
            compiler_params=pltpu.CompilerParams(vmem_limit_bytes=58 << 20),
        )(grads, turns, weighed, done)
    )


def solution(mesh):
    spec = P("dp", "seq", None)
    return jax.shard_map(
        functools.partial(local, mesh.shape["dp"], mesh.shape["seq"]),
        mesh=mesh,
        in_specs=(spec, spec, spec, spec, spec, P("dp", "seq"), P("dp")),
        out_specs=(spec, spec, spec),
        check_vma=False,
    )
```
